32 devices in a mesh: dp: 4 (over y, x), tensor: 8 (over z, core).
Axes of the slice: x: 2, y: 2, z: 4, core: 2. Of those that a mesh axis runs over, the one named last changes fastest.
Arguments:
- enc_tokens: bfloat16 [32, 128, 1024], P(('dp', 'tensor')), may hold values from -6 to 6
- src_lengths: int32 [32], replicated, may hold values from 1 to 128, as said below
- enc_gain: float32 [1024], replicated, may hold values from 0.1 to 1.9
- enc_query: bfloat16 [1024, 8192], P(None, 'tensor'), may hold values from -0.1875 to 0.1875
- enc_key: bfloat16 [1024, 8192], P(None, 'tensor'), may hold values from -0.1875 to 0.1875
- enc_value: bfloat16 [1024, 8192], P(None, 'tensor'), may hold values from -0.1875 to 0.1875
- enc_output: bfloat16 [8192, 1024], P('tensor'), may hold values from -0.0625 to 0.0625
- enc_bias: float32 [64, 33], P('tensor'), may hold values from -3 to 260
- mem_gain: float32 [1024], replicated, may hold values from 0.1 to 1.9
- dec_tokens: bfloat16 [32, 64, 1024], P(('dp', 'tensor')), may hold values from -6 to 6
- tgt_lengths: int32 [32], P(('dp', 'tensor')), may hold values from 1 to 64
- lang_tags: int32 [32], P('dp'), may hold values from 0 to 7
- lang_table: bfloat16 [8, 1024], replicated, may hold values from -6 to 6
- cross_gain: float32 [1024], replicated, may hold values from 0.1 to 1.9
- cross_query: bfloat16 [1024, 8192], P(None, 'tensor'), may hold values from -0.1875 to 0.1875
- cross_key: bfloat16 [1024, 8192], P(None, 'tensor'), may hold values from -0.1875 to 0.1875
- cross_value: bfloat16 [1024, 8192], P(None, 'tensor'), may hold values from -0.1875 to 0.1875
- cross_output: bfloat16 [8192, 1024], P('tensor'), may hold values from -0.0625 to 0.0625
- ffn_gain: float32 [1024], replicated, may hold values from 0.1 to 1.9
- ffn_in: bfloat16 [1024, 32768], P(None, 'tensor'), may hold values from -0.1875 to 0.1875
- ffn_out: bfloat16 [32768, 1024], P('tensor'), may hold values from -0.03125 to 0.03125
Outputs:
- enc_memory: bfloat16 [32, 128, 1024], P(('dp', 'tensor'))
- dec_out: bfloat16 [32, 64, 1024], P(('dp', 'tensor'))
The draws below stay inside these ranges and needn't reach their ends.
Inputs may be any that keep to these rules, and one draw needn't show every extreme that they name: `src_lengths`: never falling along the batch; the first is 1 and the last is 128.
All inputs are finite; a program needn't handle non-finite values.
Results may differ from the reference program's by a relative error of at most 0.014.
Values may be sent and summed in bfloat16 or wider, within the bound.
No kernel may reach another device: no remote copies, remote signals or barrier semaphores. Data moves between devices by JAX's collectives and lax.ppermute only.
A program may use at most 128 MiB of HBM per device.

```python
import jax
import jax.numpy as jnp
from jax import lax

D = 1024
HD = 128
HEADS = 64
FF = 32768
SRC = 128
TGT = 64
MAXREL = 16
NB = 33
LANGS = 8
PER_PAIR = 2
BATCH = 32
N_DP = 4
N_TENSOR = 8


def bias_draw(key):
    base_key = jax.random.fold_in(key, 0)
    return jnp.clip(jax.random.normal(base_key, (HEADS, NB), jnp.float32), -3.0, 3.0)


def draw_enc_bias(key, part):
    return bias_draw(jax.random.fold_in(key, 11))


def draw_src_lengths(key, part):
    drawn = jax.random.randint(jax.random.fold_in(key, 5), (BATCH,), 1, SRC + 1)
    ordered = jnp.sort(drawn)
    return ordered.at[0].set(1).at[BATCH - 1].set(SRC)


def touch_ends(entries, stream_key, least, top_value):
    index_at = [jax.random.randint(jax.random.fold_in(stream_key, axis), (), 0, length) for axis, length in enumerate(entries.shape)]
    widest = entries.shape.index(max(entries.shape))
    beside = index_at[:widest] + [(index_at[widest] + 1) % entries.shape[widest]] + index_at[widest + 1:]
    return entries.at[tuple(index_at)].set(least).at[tuple(beside)].set(top_value)


def shard_levels(key, dims, pieces, smallest, top_value):
    def one(dim, parts):
        draws = jax.random.uniform(jax.random.fold_in(jax.random.fold_in(key, 6), dim), (parts,), jnp.float32, smallest / len(pieces), top_value / len(pieces))
        return jnp.repeat(jnp.exp(draws), dims[dim] // parts).reshape((-1,) + (1,) * (len(dims) - dim - 1))

    loudness = one(*pieces[0])
    for cut in pieces[1:]:
        loudness = loudness * one(*cut)
    return loudness


def scatter_about(stream_key, dims, width, reach, pieces=(), held_as=jnp.bfloat16):
    array = jax.random.normal(stream_key, dims, jnp.float32) * width
    if len(pieces) > 0:
        array = shard_levels(stream_key, dims, pieces, -0.22, 0.18) * array
    return jnp.clip(array, min=-reach, max=reach).astype(held_as)


def setup_inputs(seed: int = 0) -> dict:
    streams_of = jax.random.split(jax.random.key(seed), 22)
    enc_tokens = scatter_about(streams_of[0], (BATCH, SRC, D), 1.0, 6.0, ((0, 32),))
    src_lengths = draw_src_lengths(jax.random.fold_in(streams_of[21], 71), 0)
    enc_gain = jnp.clip(1.0 + 0.18 * jax.random.normal(streams_of[2], (D,), jnp.float32), 0.1, 1.9)
    enc_query = scatter_about(streams_of[3], (D, HEADS * HD), D ** -0.5, 0.1875, ((1, 8),))
    enc_key = scatter_about(streams_of[4], (D, HEADS * HD), D ** -0.5, 0.1875, ((1, 8),))
    enc_value = scatter_about(streams_of[5], (D, HEADS * HD), D ** -0.5, 0.1875, ((1, 8),))
    enc_output = scatter_about(streams_of[6], (HEADS * HD, D), (HEADS * HD) ** -0.5, 0.0625, ((0, 8),))
    enc_bias = draw_enc_bias(jax.random.fold_in(streams_of[21], 71), 0)
    mem_gain = jnp.clip(1.0 + 0.18 * jax.random.normal(streams_of[8], (D,), jnp.float32), 0.1, 1.9)
    dec_tokens = scatter_about(streams_of[9], (BATCH, TGT, D), 1.0, 6.0, ((0, 32),))
    tgt_lengths = touch_ends(jax.random.randint(streams_of[10], (BATCH,), 1, TGT + 1), jax.random.fold_in(streams_of[10], 1), 1, TGT).astype(jnp.int32)
    lang_tags = touch_ends(jax.random.randint(streams_of[11], (BATCH,), 0, LANGS), jax.random.fold_in(streams_of[11], 1), 0, LANGS - 1).astype(jnp.int32)
    lang_table = scatter_about(streams_of[12], (LANGS, D), 1.0, 6.0)
    cross_gain = jnp.clip(1.0 + 0.18 * jax.random.normal(streams_of[13], (D,), jnp.float32), 0.1, 1.9)
    cross_query = scatter_about(streams_of[14], (D, HEADS * HD), D ** -0.5, 0.1875, ((1, 8),))
    cross_key = scatter_about(streams_of[15], (D, HEADS * HD), D ** -0.5, 0.1875, ((1, 8),))
    cross_value = scatter_about(streams_of[16], (D, HEADS * HD), D ** -0.5, 0.1875, ((1, 8),))
    cross_output = scatter_about(streams_of[17], (HEADS * HD, D), (HEADS * HD) ** -0.5, 0.0625, ((0, 8),))
    ffn_gain = jnp.clip(1.0 + 0.18 * jax.random.normal(streams_of[18], (D,), jnp.float32), 0.1, 1.9)
    ffn_in = scatter_about(streams_of[19], (D, FF), D ** -0.5, 0.1875, ((1, 8),))
    ffn_out = scatter_about(streams_of[20], (FF, D), FF ** -0.5, 0.03125, ((0, 8),))
    return dict(enc_tokens=enc_tokens, src_lengths=src_lengths, enc_gain=enc_gain, enc_query=enc_query, enc_key=enc_key, enc_value=enc_value, enc_output=enc_output, enc_bias=enc_bias, mem_gain=mem_gain, dec_tokens=dec_tokens, tgt_lengths=tgt_lengths, lang_tags=lang_tags, lang_table=lang_table, cross_gain=cross_gain, cross_query=cross_query, cross_key=cross_key, cross_value=cross_value, cross_output=cross_output, ffn_gain=ffn_gain, ffn_in=ffn_in, ffn_out=ffn_out)


EPSILON = 1e-06
NEG_FILL = -1e+30

def rms_norm(values, norm_gain):
    mean_sq = lax.optimization_barrier(jnp.mean(values * values, axis=-1, keepdims=True))
    return values * lax.rsqrt(mean_sq + EPSILON) * norm_gain

def make_grid(bias_table, query_len, key_len):
    offset = jnp.arange(key_len)[None, :] - jnp.arange(query_len)[:, None]
    bucket = (jnp.clip(offset, -MAXREL, MAXREL) + MAXREL).reshape(1, query_len * key_len)
    onehot = (bucket == jnp.arange(NB)[:, None]).astype(jnp.float32)
    flat_grid = jnp.dot(bias_table, onehot, precision=lax.Precision.HIGHEST, preferred_element_type=jnp.float32)
    return flat_grid.reshape(bias_table.shape[0], query_len, key_len)

def project(rows, weight):
    return jnp.dot(rows, weight, preferred_element_type=jnp.float32).astype(jnp.bfloat16)

def attend_all(query_flat, key_flat, value_flat, bias_table, lengths, query_len, key_len):
    examples = lengths.shape[0]
    query_heads = query_flat.reshape(examples, query_len, HEADS, HD)
    key_heads = key_flat.reshape(examples, key_len, HEADS, HD)
    value_heads = value_flat.reshape(examples, key_len, HEADS, HD)
    if bias_table is None:
        bias_grid = jnp.zeros((HEADS, query_len, key_len), jnp.float32)
    else:
        bias_grid = make_grid(bias_table, query_len, key_len)

    def one_example(example_item):
        query_part, key_part, value_part, length = example_item
        scores = jnp.einsum('qhd,khd->hqk', query_part.astype(jnp.float32), key_part.astype(jnp.float32), precision=lax.Precision.HIGHEST)
        scores = scores * HD ** (-0.5) + bias_grid
        key_valid = jnp.arange(key_len) < length
        scores = jnp.where(key_valid[None, None, :], scores, NEG_FILL)
        row_max = lax.optimization_barrier(jnp.max(scores, axis=-1, keepdims=True))
        exponent = jnp.exp(scores - row_max)
        weights = (exponent / lax.optimization_barrier(jnp.sum(exponent, axis=-1, keepdims=True))).astype(jnp.bfloat16)
        context = jnp.einsum('hqk,khd->qhd', weights.astype(jnp.float32), value_part.astype(jnp.float32), precision=lax.Precision.HIGHEST)
        return context.astype(jnp.bfloat16)
    contexts = lax.map(one_example, (query_heads, key_heads, value_heads, lengths))
    return contexts.reshape(examples * query_len, HEADS * HD)

def group_sum(context, weight):
    group_width = context.shape[1] // N_TENSOR

    def add_group(running, group_index):
        first_row = (group_index * group_width).astype(jnp.int32)
        context_part = lax.dynamic_slice_in_dim(context, first_row, group_width, 1)
        rows_part = lax.dynamic_slice_in_dim(weight, first_row, group_width, 0)
        partial_value = jnp.dot(context_part, rows_part, preferred_element_type=jnp.float32).astype(jnp.bfloat16)
        partial_value = lax.optimization_barrier(partial_value)
        return (running + partial_value.astype(jnp.float32), None)
    start_value = jnp.zeros((context.shape[0], weight.shape[1]), jnp.float32)
    summed, _ = lax.scan(add_group, start_value, jnp.arange(N_TENSOR, dtype=jnp.int32))
    return summed

def ffn_sum(normed, weight_in, weight_out):
    group_width = weight_in.shape[1] // N_TENSOR

    def add_group(running, group_index):
        first_row = (group_index * group_width).astype(jnp.int32)
        in_cols = lax.dynamic_slice_in_dim(weight_in, first_row, group_width, 1)
        activated = jnp.maximum(jnp.dot(normed, in_cols, preferred_element_type=jnp.float32), 0.0).astype(jnp.bfloat16)
        out_rows = lax.dynamic_slice_in_dim(weight_out, first_row, group_width, 0)
        partial_value = jnp.dot(activated, out_rows, preferred_element_type=jnp.float32).astype(jnp.bfloat16)
        partial_value = lax.optimization_barrier(partial_value)
        return (running + partial_value.astype(jnp.float32), None)
    start_value = jnp.zeros((normed.shape[0], weight_out.shape[1]), jnp.float32)
    summed, _ = lax.scan(add_group, start_value, jnp.arange(N_TENSOR, dtype=jnp.int32))
    return summed

def restripe(values):
    shaped = values.reshape((N_DP, PER_PAIR, N_DP) + values.shape[1:])
    axes_order = (2, 0, 1) + tuple(range(3, shaped.ndim))
    return jnp.transpose(shaped, axes_order).reshape(values.shape)

def reference(enc_tokens, src_lengths, enc_gain, enc_query, enc_key, enc_value, enc_output, enc_bias, mem_gain, dec_tokens, tgt_lengths, lang_tags, lang_table, cross_gain, cross_query, cross_key, cross_value, cross_output, ffn_gain, ffn_in, ffn_out):
    examples = enc_tokens.shape[0]
    enc_input = enc_tokens.astype(jnp.float32).reshape(examples * SRC, D)
    enc_normed = rms_norm(enc_input, enc_gain).astype(jnp.bfloat16)
    enc_context = attend_all(project(enc_normed, enc_query), project(enc_normed, enc_key), project(enc_normed, enc_value), enc_bias, src_lengths, SRC, SRC)
    enc_hidden = enc_input + group_sum(enc_context, enc_output)
    enc_memory = rms_norm(enc_hidden, mem_gain).astype(jnp.bfloat16)
    dec_memory = restripe(enc_memory.reshape(examples, SRC, D)).reshape(examples * SRC, D)
    dec_src_len = restripe(src_lengths)
    lang_rows = lang_table[lang_tags].astype(jnp.float32)
    dec_input = (dec_tokens.astype(jnp.float32) + lang_rows[:, None, :]).reshape(examples * TGT, D)
    dec_normed = rms_norm(dec_input, cross_gain).astype(jnp.bfloat16)
    cross_context = attend_all(project(dec_normed, cross_query), project(dec_memory, cross_key), project(dec_memory, cross_value), None, dec_src_len, TGT, SRC)
    hidden_state = dec_input + group_sum(cross_context, cross_output)
    ffn_normed = rms_norm(hidden_state, ffn_gain).astype(jnp.bfloat16)
    dec_full = hidden_state + ffn_sum(ffn_normed, ffn_in, ffn_out)
    keep = jnp.arange(TGT)[None, :] < tgt_lengths[:, None]
    dec_out = jnp.where(keep[:, :, None], dec_full.reshape(examples, TGT, D), 0.0).astype(jnp.bfloat16)
    return (enc_memory.reshape(examples, SRC, D), dec_out)
```

```python
import functools

import jax
import jax.numpy as jnp
from jax import lax
from jax.experimental import pallas as pl
from jax.experimental.pallas import tpu as pltpu
from jax.sharding import PartitionSpec as P

HD = 128
MAXREL = 16
NB = 33
EPSILON = 1e-06
NEG_FILL = -1e30
HEADS_STEP = 4
FFN_STEP = 512
OUT_STEP = 256
VMEM_LIMIT = 16 * 1024 * 1024

BF16 = jnp.bfloat16
F32 = jnp.float32


def rms_norm(values, norm_gain):
    mean_sq = jnp.mean(values * values, axis=-1, keepdims=True)
    return values * lax.rsqrt(mean_sq + EPSILON) * norm_gain


def make_grid(bias_table, query_len, key_len):
    offset = jnp.arange(key_len)[None, :] - jnp.arange(query_len)[:, None]
    bucket = (jnp.clip(offset, -MAXREL, MAXREL) + MAXREL).reshape(1, query_len * key_len)
    onehot = (bucket == jnp.arange(NB)[:, None]).astype(F32)
    flat_grid = jnp.dot(
        bias_table, onehot, precision=lax.Precision.HIGHEST, preferred_element_type=F32
    )
    return flat_grid.reshape(bias_table.shape[0], query_len, key_len)


def dot(a, b):
    return jnp.dot(a, b, preferred_element_type=F32)


def softmax_contexts(query, key, value, bias, masks, parts):
    query_len, key_len = query.shape[0] // parts, key.shape[0] // parts
    ones = jnp.ones((key_len, HD), BF16)
    examples = []
    for i in range(parts):
        rows_q = slice(i * query_len, (i + 1) * query_len)
        rows_k = slice(i * key_len, (i + 1) * key_len)
        heads = []
        for h in range(query.shape[1] // HD):
            columns = slice(h * HD, (h + 1) * HD)
            scores = lax.dot_general(
                query[rows_q, columns], key[rows_k, columns], (((1,), (1,)), ((), ())),
                preferred_element_type=F32,
            )
            scores = scores * HD ** (-0.5)
            if bias is not None:
                scores = scores + bias(h)
            scores = jnp.where(masks[i], scores, NEG_FILL)
            row_max = jnp.max(scores, axis=-1, keepdims=True)
            exponent = jnp.exp(scores - row_max).astype(BF16)
            summed = dot(exponent, jnp.concatenate([value[rows_k, columns], ones], axis=1))
            heads.append((summed[:, :HD] / summed[:, HD:]).astype(BF16))
        examples.append(jnp.concatenate(heads, axis=1))
    return jnp.concatenate(examples, axis=0)


def attention_body(has_bias, parts, *refs):
    refs = list(refs)
    lens = refs.pop(0)
    key_parts = [refs.pop(0) for _ in range(parts)]
    query_parts = key_parts if has_bias else [refs.pop(0) for _ in range(parts)]
    wq, wk, wv, wo = [refs.pop(0) for _ in range(4)]
    bias = refs.pop(0) if has_bias else None
    outs = [refs.pop(0) for _ in range(parts)]
    (context,) = refs
    key_len, query_len = key_parts[0].shape[0], query_parts[0].shape[0]
    key_rows = jnp.concatenate([ref[...] for ref in key_parts], axis=0)
    query_rows = key_rows
    if not has_bias:
        query_rows = jnp.concatenate([ref[...] for ref in query_parts], axis=0)
    key_index = lax.broadcasted_iota(jnp.int32, (query_len, key_len), 1)
    masks = [key_index < lens[i] for i in range(parts)]
    columns = wq.shape[1]
    block = min(HEADS_STEP * HD, columns)
    for start in range(0, columns, block):
        cols = slice(start, start + block)
        keys = dot(key_rows, wk[:, cols]).astype(BF16)
        values = dot(key_rows, wv[:, cols]).astype(BF16)
        queries = dot(query_rows, wq[:, cols]).astype(BF16)
        head_bias = None
        if has_bias:
            head_bias = lambda h, first=start // HD: bias[first + h]
        context[:, cols] = softmax_contexts(queries, keys, values, head_bias, masks, parts)
    term = dot(context[...], wo[...]).astype(BF16)
    for i in range(parts):
        outs[i][...] = term[i * query_len:(i + 1) * query_len]


IN_VMEM = pl.BlockSpec(memory_space=pltpu.VMEM)


def attention(lens, key_parts, query_parts, wq, wk, wv, wo, bias):
    parts = len(key_parts)
    key_len, width = key_parts[0].shape
    query_len = query_parts[0].shape[0] if query_parts else key_len
    columns = wq.shape[1]
    has_bias = bias is not None
    operands = list(key_parts)
    if query_parts:
        operands += list(query_parts)
    operands += [wq, wk, wv, wo]
    if has_bias:
        operands += [bias]
    rows_q, rows_k = parts * query_len, parts * key_len
    return pl.pallas_call(
        functools.partial(attention_body, has_bias, parts),
        in_specs=[pl.BlockSpec(memory_space=pltpu.SMEM)] + [IN_VMEM] * len(operands),
        out_specs=[IN_VMEM] * parts,
        out_shape=[jax.ShapeDtypeStruct((query_len, width), BF16)] * parts,
        scratch_shapes=[pltpu.VMEM((rows_q, columns), BF16)],
        compiler_params=pltpu.CompilerParams(vmem_limit_bytes=VMEM_LIMIT),
        cost_estimate=pl.CostEstimate(
            flops=4 * width * columns * (rows_q + rows_k) + 4 * rows_q * key_len * columns,
            bytes_accessed=8 * width * columns + 4 * width * (rows_q + rows_k),
            transcendentals=rows_q * key_len * columns // HD,
        ),
        name="enc_attention" if has_bias else "cross_attention",
    )(lens, *operands)


def ffn_body(parts, *refs):
    row_parts = refs[:parts]
    w_in, w_out = refs[parts:parts + 2]
    outs = refs[parts + 2:2 * parts + 2]
    (activated,) = refs[2 * parts + 2:]
    part_len = row_parts[0].shape[0]
    rows = jnp.concatenate([ref[...] for ref in row_parts], axis=0)
    block = min(FFN_STEP, w_in.shape[1])
    for start in range(0, w_in.shape[1], block):
        cols = slice(start, start + block)
        activated[:, cols] = jnp.maximum(dot(rows, w_in[:, cols]), 0.0).astype(BF16)
    block = min(OUT_STEP, w_out.shape[1])
    for start in range(0, w_out.shape[1], block):
        cols = slice(start, start + block)
        term = dot(activated[...], w_out[:, cols]).astype(BF16)
        for i in range(parts):
            outs[i][:, cols] = term[i * part_len:(i + 1) * part_len]


def ffn(row_parts, w_in, w_out):
    parts = len(row_parts)
    part_len, width = row_parts[0].shape
    hidden = w_in.shape[1]
    rows = parts * part_len
    return pl.pallas_call(
        functools.partial(ffn_body, parts),
        in_specs=[IN_VMEM] * (parts + 2),
        out_specs=[IN_VMEM] * parts,
        out_shape=[jax.ShapeDtypeStruct((part_len, width), BF16)] * parts,
        scratch_shapes=[pltpu.VMEM((rows, hidden), BF16)],
        compiler_params=pltpu.CompilerParams(vmem_limit_bytes=VMEM_LIMIT),
        cost_estimate=pl.CostEstimate(
            flops=4 * rows * width * hidden,
            bytes_accessed=4 * width * hidden + 4 * rows * width,
            transcendentals=0,
        ),
        name="feed_forward",
    )(*row_parts, w_in, w_out)


def swap(value, bits):
    size = lax.axis_size("tensor")
    return lax.ppermute(value, "tensor", [(i, i ^ bits) for i in range(size)])


def spread(block):
    size = lax.axis_size("tensor")
    slots = {0: block}
    bit = size // 2
    while bit >= 1:
        for k in sorted(slots):
            slots[k ^ bit] = swap(slots[k], bit)
        bit //= 2
    return [slots[k] for k in range(size)]


def gather_sum(pairs, direct):
    count = len(pairs)
    own = [pairs[0][0], swap(pairs[0][1], 1)]
    sums = {k: [pairs[k][0], swap(pairs[k][1], 1)] for k in range(1, count)}

    def total(terms):
        result = terms[0].astype(F32)
        for term in terms[1:]:
            result = result + term.astype(F32)
        return result.astype(BF16)

    if direct:
        for k in range(count - 1, 0, -1):
            own.append(swap(total(sums[k]), 2 * k))
        return own
    bit = 1
    while bit < count:
        for k in range(count - 1, 0, -1):
            if k & bit and not k & (bit - 1):
                arrived = swap(total(sums[k]), 2 * bit)
                if k == bit:
                    own.append(arrived)
                else:
                    sums[k ^ bit].append(arrived)
        bit *= 2
    return own


def norm_body(count, with_sum, *refs):
    addends = refs[:count]
    gain = refs[count]
    outs = refs[count + 1:]
    total = addends[0][...].astype(F32)
    for ref in addends[1:]:
        total = total + ref[...].astype(F32)
    mean_sq = jnp.mean(total * total, axis=-1, keepdims=True)
    outs[0][...] = (total * lax.rsqrt(mean_sq + EPSILON) * gain[...]).astype(BF16)
    if with_sum:
        outs[1][...] = total


def norm_sum(addends, gain, with_sum):
    rows, width = addends[0].shape
    out_shape = [jax.ShapeDtypeStruct((rows, width), BF16)]
    if with_sum:
        out_shape.append(jax.ShapeDtypeStruct((rows, width), F32))
    return pl.pallas_call(
        functools.partial(norm_body, len(addends), with_sum),
        out_shape=out_shape,
        compiler_params=pltpu.CompilerParams(vmem_limit_bytes=VMEM_LIMIT),
        cost_estimate=pl.CostEstimate(
            flops=8 * rows * width,
            bytes_accessed=2 * rows * width * (len(addends) + 3),
            transcendentals=rows,
        ),
        name="sum_norm",
    )(*addends, gain[None, :])


def on_device(
    enc_tokens,
    src_lengths,
    enc_gain,
    enc_query,
    enc_key,
    enc_value,
    enc_output,
    enc_bias,
    mem_gain,
    dec_tokens,
    tgt_lengths,
    lang_tags,
    lang_table,
    cross_gain,
    cross_query,
    cross_key,
    cross_value,
    cross_output,
    ffn_gain,
    ffn_in,
    ffn_out,
):
    groups = lax.axis_size("dp")
    size = lax.axis_size("tensor")
    group_index = lax.axis_index("dp")
    tensor_index = lax.axis_index("tensor")
    per_pair = size // groups
    src_len = enc_tokens.shape[1]
    target_len = dec_tokens.shape[1]

    to_source = []
    for row in range(groups * size):
        j, m = row // size, row % size
        to_source.append((row, (m // per_pair) * size + (m % per_pair) * groups + j))
    to_home = [(b, a) for a, b in to_source]

    slot_ids = tensor_index ^ jnp.arange(size)
    lens = src_lengths[group_index * size + slot_ids]

    (enc_normed,) = norm_sum([enc_tokens[0]], enc_gain, False)
    enc_slots = spread(enc_normed)
    bias = make_grid(enc_bias, src_len, src_len)
    enc_pairs = []
    for k in range(size // 2):
        enc_pairs.append(
            attention(
                lens[2 * k:2 * k + 2], enc_slots[2 * k:2 * k + 2], None,
                enc_query, enc_key, enc_value, enc_output, bias,
            )
        )
    enc_terms = gather_sum(enc_pairs, True)
    (enc_memory,) = norm_sum([enc_tokens[0]] + enc_terms, mem_gain, False)

    tag = lax.dynamic_index_in_dim(lang_tags, tensor_index, keepdims=False)
    lang_row = lax.dynamic_slice_in_dim(lang_table, tag, 1, 0)
    sent = jnp.concatenate([dec_tokens[0], jnp.broadcast_to(lang_row, (16, lang_row.shape[1]))])
    arrived = lax.ppermute(sent, ("dp", "tensor"), to_source)
    dec_rows = arrived[:target_len]
    dec_lang = jnp.broadcast_to(arrived[target_len:target_len + 1], dec_rows.shape)
    dec_normed, dec_input = norm_sum([dec_rows, dec_lang], cross_gain, True)
    dec_slots = spread(dec_normed)

    mem_slots = spread(enc_memory)
    cross_pairs = []
    for k in range(size // 2):
        cross_pairs.append(
            attention(
                lens[2 * k:2 * k + 2], mem_slots[2 * k:2 * k + 2], dec_slots[2 * k:2 * k + 2],
                cross_query, cross_key, cross_value, cross_output, None,
            )
        )
    cross_terms = gather_sum(cross_pairs, True)
    ffn_normed, hidden = norm_sum([dec_input] + cross_terms, ffn_gain, True)

    ffn_slots = spread(ffn_normed)
    ffn_pairs = []
    for k in range(size // 2):
        ffn_pairs.append(ffn(ffn_slots[2 * k:2 * k + 2], ffn_in, ffn_out))
    ffn_terms = gather_sum(ffn_pairs, True)
    dec_sum = hidden
    for term in ffn_terms:
        dec_sum = dec_sum + term.astype(F32)
    dec_home = lax.ppermute(dec_sum.astype(BF16), ("dp", "tensor"), to_home)
    keep = jnp.arange(target_len)[:, None] < tgt_lengths[0]
    dec_out = jnp.where(keep, dec_home, jnp.zeros_like(dec_home))
    return (enc_memory[None], dec_out[None])


def solution(mesh):
    in_specs = (
        P(("dp", "tensor"), None, None),
        P(),
        P(),
        P(None, "tensor"),
        P(None, "tensor"),
        P(None, "tensor"),
        P("tensor", None),
        P("tensor", None),
        P(),
        P(("dp", "tensor"), None, None),
        P(("dp", "tensor")),
        P("dp"),
        P(),
        P(),
        P(None, "tensor"),
        P(None, "tensor"),
        P(None, "tensor"),
        P("tensor", None),
        P(),
        P(None, "tensor"),
        P("tensor", None),
    )
    out_specs = (P(("dp", "tensor"), None, None), P(("dp", "tensor"), None, None))
    return jax.shard_map(
        on_device, mesh=mesh, in_specs=in_specs, out_specs=out_specs, check_vma=False
    )
```

```python
import functools

import jax
import jax.numpy as jnp
from jax import lax
from jax.experimental import pallas as pl
from jax.experimental.pallas import tpu as pltpu
from jax.sharding import PartitionSpec as P

HD = 128
MAXREL = 16
NB = 33
LANG_ROWS = 16
TIE_OWN = True
TIE_NEAR = False
EPSILON = 1e-06
NEG_FILL = -1e30
FFN_STEP = 512
OUT_STEP = 256
VMEM_LIMIT = 16 * 1024 * 1024

IN_VMEM = pl.BlockSpec(memory_space=pltpu.VMEM)
IN_HBM = pl.BlockSpec(memory_space=pltpu.HBM)
IN_SMEM = pl.BlockSpec(memory_space=pltpu.SMEM)
BF16 = jnp.bfloat16
F32 = jnp.float32


def rms_norm(values, norm_gain):
    mean_sq = jnp.mean(values * values, axis=-1, keepdims=True)
    return values * lax.rsqrt(mean_sq + EPSILON) * norm_gain


def after(value, *earlier):
    return lax.optimization_barrier((value,) + earlier)[0]


def in_hbm(*arrays):
    return [pltpu.with_memory_space_constraint(array, pltpu.HBM) for array in arrays]


def load_body(count, *refs):
    sources = refs[:count + 1]
    targets, bias = refs[count + 2:2 * count + 2], refs[2 * count + 2]
    table, sems = refs[2 * count + 3:]
    copies = [
        pltpu.make_async_copy(source, target, sems.at[i])
        for i, (source, target) in enumerate(zip(sources, [*targets, table]))
    ]
    for copy in copies[::-1]:
        copy.start()
    copies.pop().wait()
    heads, query_len, key_len = bias.shape
    shape = (query_len, key_len)
    offset = lax.broadcasted_iota(jnp.int32, shape, 1) - lax.broadcasted_iota(jnp.int32, shape, 0)
    bucket = jnp.clip(offset, -MAXREL, MAXREL) + MAXREL
    for h in range(heads):
        grid = jnp.full(shape, table[h, 0], F32)
        for n in range(1, NB):
            grid = jnp.where(bucket == n, table[h, n], grid)
        bias[h] = grid
    for copy in copies:
        copy.wait()


def load(weights, bias_table, query_len, key_len, earlier):
    count = len(weights)
    heads = bias_table.shape[0]
    size = sum(w.size * w.dtype.itemsize for w in weights)
    return pl.pallas_call(
        functools.partial(load_body, count),
        in_specs=[IN_HBM] * (count + 1) + [IN_VMEM],
        out_specs=[IN_VMEM] * (count + 1),
        out_shape=[jax.ShapeDtypeStruct(w.shape, w.dtype) for w in weights]
        + [jax.ShapeDtypeStruct((heads, query_len, key_len), F32)],
        scratch_shapes=[
            pltpu.SMEM(bias_table.shape, bias_table.dtype),
            pltpu.SemaphoreType.DMA((count + 1,)),
        ],
        compiler_params=pltpu.CompilerParams(vmem_limit_bytes=VMEM_LIMIT),
        cost_estimate=pl.CostEstimate(flops=0, bytes_accessed=2 * size, transcendentals=0),
        name="load",
    )(*in_hbm(*weights, bias_table), earlier)


def dot(a, b):
    return jnp.dot(a, b, preferred_element_type=F32)


def softmax_contexts(query, key, value, bias, masks, parts):
    query_len, key_len = query.shape[0] // parts, key.shape[0] // parts
    ones = jnp.ones((key_len, HD), BF16)
    units = [(i, h) for i in range(parts) for h in range(query.shape[1] // HD)]

    def take(rows, length, unit):
        i, h = unit
        return rows[i * length:(i + 1) * length, h * HD:(h + 1) * HD]

    scores = [
        lax.dot_general(
            take(query, query_len, unit), take(key, key_len, unit), (((1,), (1,)), ((), ())),
            preferred_element_type=F32,
        )
        for unit in units
    ]
    scores = [score * HD ** (-0.5) for score in scores]
    if bias is not None:
        scores = [score + bias[h] for (_, h), score in zip(units, scores)]
    scores = [jnp.where(masks[i], score, NEG_FILL) for (i, _), score in zip(units, scores)]
    row_max = [jnp.max(score, axis=-1, keepdims=True) for score in scores]
    exponent = [jnp.exp(score - top).astype(BF16) for score, top in zip(scores, row_max)]
    summed = [
        dot(part, jnp.concatenate([take(value, key_len, unit), ones], axis=1))
        for unit, part in zip(units, exponent)
    ]
    context = [(total[:, :HD] / total[:, HD:]).astype(BF16) for total in summed]
    heads = len(units) // parts
    return jnp.concatenate(
        [jnp.concatenate(context[i * heads:(i + 1) * heads], axis=1) for i in range(parts)], axis=0
    )


def attention_body(has_bias, parts, first_slot, size, *refs):
    refs = list(refs)
    lengths = refs.pop(0)
    key_parts = [refs.pop(0) for _ in range(parts)]
    queries_in = [] if has_bias else [refs.pop(0), refs.pop(0)]
    wq, wk, wv, wo = [refs.pop(0) for _ in range(4)]
    bias = refs.pop(0) if has_bias else None
    outs = refs
    key_len, query_len = key_parts[0].shape[0], outs[0].shape[0]
    key_rows = jnp.concatenate([ref[...] for ref in key_parts], axis=0)
    query_rows = key_rows
    first = lax.axis_index("dp") * size
    here = lax.axis_index("tensor")
    if not has_bias:
        query_rows = jnp.concatenate(
            [queries_in[i][first_slot // 2] for i in range(parts)], axis=0
        )
    key_index = lax.broadcasted_iota(jnp.int32, (query_len, key_len), 1)
    masks = [key_index < lengths[first + (here ^ (first_slot + i))] for i in range(parts)]
    keys = dot(key_rows, wk[...]).astype(BF16)
    values = dot(key_rows, wv[...]).astype(BF16)
    queries = dot(query_rows, wq[...]).astype(BF16)
    context = softmax_contexts(queries, keys, values, bias, masks, parts)
    term = dot(context, wo[...]).astype(BF16)
    for i in range(parts):
        outs[i][...] = term[i * query_len:(i + 1) * query_len]


def attention(lengths, first_slot, key_parts, queries_in, wq, wk, wv, wo, bias):
    parts = len(key_parts)
    key_len, width = key_parts[0].shape
    query_len = queries_in[0].shape[1] if queries_in else key_len
    columns = wq.shape[1]
    has_bias = bias is not None
    operands = list(key_parts)
    if queries_in:
        operands += queries_in
    operands += [wq, wk, wv, wo]
    if has_bias:
        operands += [bias]
    rows_q, rows_k = parts * query_len, parts * key_len
    return pl.pallas_call(
        functools.partial(
            attention_body, has_bias, parts, first_slot, lax.axis_size("tensor")
        ),
        in_specs=[IN_SMEM] + [IN_VMEM] * len(operands),
        out_specs=[IN_VMEM] * parts,
        out_shape=[jax.ShapeDtypeStruct((query_len, width), BF16)] * parts,
        compiler_params=pltpu.CompilerParams(vmem_limit_bytes=VMEM_LIMIT),
        cost_estimate=pl.CostEstimate(
            flops=4 * width * columns * (rows_q + rows_k) + 4 * rows_q * key_len * columns,
            bytes_accessed=4 * width * (rows_q + rows_k),
            transcendentals=0,
        ),
        name="enc_attention" if has_bias else "cross_attention",
    )(lengths, *operands)


def ffn_body(parts, *refs):
    row_parts = refs[:parts]
    w_in, w_out = refs[parts:parts + 2]
    outs = refs[parts + 2:2 * parts + 2]
    (activated,) = refs[2 * parts + 2:]
    part_len = row_parts[0].shape[0]
    rows = jnp.concatenate([ref[...] for ref in row_parts], axis=0)
    block = min(FFN_STEP, w_in.shape[1])
    for start in range(0, w_in.shape[1], block):
        cols = slice(start, start + block)
        activated[:, cols] = jnp.maximum(dot(rows, w_in[:, cols]), 0.0).astype(BF16)
    block = min(OUT_STEP, w_out.shape[1])
    for start in range(0, w_out.shape[1], block):
        cols = slice(start, start + block)
        term = dot(activated[...], w_out[:, cols]).astype(BF16)
        for i in range(parts):
            outs[i][:, cols] = term[i * part_len:(i + 1) * part_len]


def ffn(row_parts, w_in, w_out):
    parts = len(row_parts)
    part_len, width = row_parts[0].shape
    hidden = w_in.shape[1]
    rows = parts * part_len
    return pl.pallas_call(
        functools.partial(ffn_body, parts),
        in_specs=[IN_VMEM] * (parts + 2),
        out_specs=[IN_VMEM] * parts,
        out_shape=[jax.ShapeDtypeStruct((part_len, width), BF16)] * parts,
        scratch_shapes=[pltpu.VMEM((rows, hidden), BF16)],
        compiler_params=pltpu.CompilerParams(vmem_limit_bytes=VMEM_LIMIT),
        cost_estimate=pl.CostEstimate(
            flops=4 * rows * width * hidden,
            bytes_accessed=4 * rows * width,
            transcendentals=0,
        ),
        name="feed_forward",
    )(*row_parts, w_in, w_out)


def swap(value, bits):
    size = lax.axis_size("tensor")
    return lax.ppermute(value, "tensor", [(i, i ^ bits) for i in range(size)])


def spread(block):
    size = lax.axis_size("tensor")
    slots = {0: block}
    bit = size // 2
    while bit > 1:
        for k in sorted(slots):
            slots[k ^ bit] = swap(slots[k], bit)
        bit //= 2
    own = jnp.stack([slots[2 * k] for k in range(size // 2)])
    return own, swap(own, 1), [slots[size // 2], slots[size // 4]]


def bf16_sum(*terms):
    total = terms[0].astype(F32)
    for term in terms[1:]:
        total = total + term.astype(F32)
    return total.astype(BF16)


def exchange(block, run, before_last=()):
    size = lax.axis_size("tensor")
    last = size // 2 - 1
    outs = {0: run(0, [block, swap(block, 1)])}
    addends = [outs[0][0], swap(outs[0][1], 1)]
    slots = {0: block}
    bit = size // 2
    while bit > 1:
        for k in sorted(slots):
            slots[k ^ bit] = swap(slots[k], bit)
        bit //= 2
        if bit > 1:
            for k in sorted(slots):
                if k:
                    slots[k] = after(slots[k], outs[0][0])
    near, held = {}, [addends[1]] if TIE_OWN else [outs[0][0]]
    for k in [*range(2, last, 2), *range(1, last + 1, 2)]:
        first = slots[2 * k]
        if k == last:
            held += before_last
        if k in near and TIE_NEAR:
            held.append(near[k])
        outs[k] = run(k, [after(first, *held), swap(after(first, *held) if k == last else first, 1)])
        held = [outs[k][0]]
        terms = [outs[k][0], swap(outs[k][1], 1)]
        if k in near:
            terms.append(near[k])
        partial_sum = bf16_sum(*terms)
        if k % 2:
            addends.append(swap(partial_sum, 2 * k))
        else:
            near[k + 1] = swap(partial_sum, 2)
    return addends


def prologue_body(tokens, gain, dec_rows, table, tags, ends, normed, sent, *scratch):
    buffers, sems = scratch[:6], scratch[6]
    copies = [
        pltpu.make_async_copy(source, target, sems.at[i])
        for i, (source, target) in enumerate(
            zip((tokens, gain, dec_rows, table, tags, ends), buffers)
        )
    ]
    for copy in copies:
        copy.start()
    for copy in copies:
        copy.wait()
    normed[...] = rms_norm(buffers[0][...].astype(F32), buffers[1][...]).astype(BF16)
    count = dec_rows.shape[0]
    sent[:count, :] = buffers[2][...]
    langs, width = table.shape
    tag = buffers[4][lax.axis_index("tensor")]
    chosen = lax.broadcasted_iota(jnp.int32, (langs, width), 0) == tag
    row = jnp.sum(jnp.where(chosen, buffers[3][...].astype(F32), 0.0), axis=0, keepdims=True)
    shape = (sent.shape[0] - count, width)
    end = jnp.full(shape, buffers[5][0], jnp.int32).astype(F32)
    is_row = lax.broadcasted_iota(jnp.int32, shape, 0) == 0
    sent[count:, :] = jnp.where(is_row, jnp.broadcast_to(row, shape), end).astype(BF16)


def prologue(tokens, gain, dec_rows, table, tags, ends):
    (rows, width), count = tokens.shape, dec_rows.shape[0]
    operands = [tokens, gain[None, :], dec_rows, table, tags, ends]
    return pl.pallas_call(
        prologue_body,
        in_specs=[IN_HBM] * 6,
        out_specs=[IN_VMEM] * 2,
        out_shape=[
            jax.ShapeDtypeStruct((rows, width), BF16),
            jax.ShapeDtypeStruct((count + LANG_ROWS, width), BF16),
        ],
        scratch_shapes=[pltpu.VMEM(x.shape, x.dtype) for x in operands[:4]]
        + [pltpu.SMEM(x.shape, x.dtype) for x in operands[4:]]
        + [pltpu.SemaphoreType.DMA((6,))],
        compiler_params=pltpu.CompilerParams(vmem_limit_bytes=VMEM_LIMIT),
        name="prologue",
    )(*in_hbm(*operands[:4]), *operands[4:])


def norm_body(count, copies, *refs):
    addends = refs[:count]
    gain = refs[count]
    outs = refs[count + 1:]
    total = addends[0][...].astype(F32)
    for ref in addends[1:]:
        total = total + ref[...].astype(F32)
    normed = rms_norm(total, gain[...]).astype(BF16)
    for ref in outs[:copies]:
        ref[...] = normed
    for ref in outs[copies:]:
        ref[...] = total


def norm_sum(addends, gain, copies, with_sum):
    rows, width = addends[0].shape
    out_shape = [jax.ShapeDtypeStruct((rows, width), BF16)] * copies
    if with_sum:
        out_shape.append(jax.ShapeDtypeStruct((rows, width), F32))
    return pl.pallas_call(
        functools.partial(norm_body, len(addends), copies),
        out_shape=out_shape,
        compiler_params=pltpu.CompilerParams(vmem_limit_bytes=VMEM_LIMIT),
        cost_estimate=pl.CostEstimate(
            flops=8 * rows * width,
            bytes_accessed=2 * rows * width * (len(addends) + 3),
            transcendentals=rows,
        ),
        name="sum_norm",
    )(*addends, gain[None, :])


def masked_body(count, *refs):
    addends, ends, out = refs[:count], refs[count], refs[count + 1]
    total = addends[0][...].astype(F32)
    for ref in addends[1:]:
        total = total + ref[...].astype(F32)
    row = lax.broadcasted_iota(jnp.int32, total.shape, 0).astype(F32)
    keep = row < ends[:, :1].astype(F32)
    out[...] = jnp.where(keep, total, 0.0).astype(BF16)


def masked_sum(addends, ends):
    rows, width = addends[0].shape
    return pl.pallas_call(
        functools.partial(masked_body, len(addends)),
        out_shape=jax.ShapeDtypeStruct((rows, width), BF16),
        compiler_params=pltpu.CompilerParams(vmem_limit_bytes=VMEM_LIMIT),
        name="masked_sum",
    )(*addends, ends)


def on_device(
    enc_tokens,
    src_lengths,
    enc_gain,
    enc_query,
    enc_key,
    enc_value,
    enc_output,
    enc_bias,
    mem_gain,
    dec_tokens,
    tgt_lengths,
    lang_tags,
    lang_table,
    cross_gain,
    cross_query,
    cross_key,
    cross_value,
    cross_output,
    ffn_gain,
    ffn_in,
    ffn_out,
):
    groups = lax.axis_size("dp")
    size = lax.axis_size("tensor")
    per_pair = size // groups
    src_len = enc_tokens.shape[1]
    target_len = dec_tokens.shape[1]

    to_source = []
    for row in range(groups * size):
        j, m = row // size, row % size
        to_source.append((row, (m // per_pair) * size + (m % per_pair) * groups + j))
    to_home = [(b, a) for a, b in to_source]

    enc_normed, sent = prologue(
        enc_tokens[0], enc_gain, dec_tokens[0], lang_table, lang_tags, tgt_lengths
    )
    *enc_weights, bias = load(
        [enc_query, enc_key, enc_value, enc_output], enc_bias, src_len, src_len, enc_normed
    )

    arrived = lax.ppermute(sent, ("dp", "tensor"), to_source)
    dec_rows = arrived[:target_len]
    dec_lang = jnp.broadcast_to(arrived[target_len:target_len + 1], dec_rows.shape)
    dec_normed, dec_input = norm_sum([dec_rows, dec_lang], cross_gain, 1, True)
    def enc_pair(k, blocks):
        return attention(src_lengths, 2 * k, blocks, None, *enc_weights, bias)

    dec_own, dec_other, early = spread(dec_normed)
    enc_terms = exchange(enc_normed, enc_pair, early)
    memory_out, enc_memory = norm_sum([enc_tokens[0]] + enc_terms, mem_gain, 2, False)

    def cross_pair(k, blocks):
        return attention(
            src_lengths, 2 * k, blocks, [dec_own, dec_other],
            cross_query, cross_key, cross_value, cross_output, None,
        )

    cross_terms = exchange(enc_memory, cross_pair)
    ffn_normed, hidden = norm_sum([dec_input] + cross_terms, ffn_gain, 1, True)

    def ffn_pair(k, blocks):
        return ffn(blocks, ffn_in, ffn_out)

    ffn_terms = exchange(ffn_normed, ffn_pair)
    ends = jnp.broadcast_to(arrived[target_len + 1:target_len + 2, :HD], (target_len, HD))
    dec_sum = masked_sum([hidden] + ffn_terms, ends)
    dec_out = lax.ppermute(dec_sum, ("dp", "tensor"), to_home)
    return (memory_out[None], dec_out[None])


def solution(mesh):
    in_specs = (
        P(("dp", "tensor"), None, None),
        P(),
        P(),
        P(None, "tensor"),
        P(None, "tensor"),
        P(None, "tensor"),
        P("tensor", None),
        P("tensor", None),
        P(),
        P(("dp", "tensor"), None, None),
        P(("dp", "tensor")),
        P("dp"),
        P(),
        P(),
        P(None, "tensor"),
        P(None, "tensor"),
        P(None, "tensor"),
        P("tensor", None),
        P(),
        P(None, "tensor"),
        P("tensor", None),
    )
    out_specs = (P(("dp", "tensor"), None, None), P(("dp", "tensor"), None, None))
    return jax.shard_map(
        on_device, mesh=mesh, in_specs=in_specs, out_specs=out_specs, check_vma=False
    )
```

```python
import functools

import jax
import jax.numpy as jnp
from jax import lax
from jax.experimental import pallas as pl
from jax.experimental.pallas import tpu as pltpu
from jax.sharding import PartitionSpec as P

HD = 128
MAXREL = 16
NB = 33
LANG_ROWS = 16
OPT = dict(enc="213", mem="213", ffn="213", p3=(), p1=(), dec="early", norm2=True, p3tie=("enc", "mem", "ffn"), straight=False, home="w", dtie=False, w="all", ls=2)
EPSILON = 1e-06
NEG_FILL = -1e30
FFN_STEP = 512
OUT_STEP = 256
VMEM_LIMIT = 16 * 1024 * 1024

IN_VMEM = pl.BlockSpec(memory_space=pltpu.VMEM)
IN_HBM = pl.BlockSpec(memory_space=pltpu.HBM)
IN_SMEM = pl.BlockSpec(memory_space=pltpu.SMEM)
BF16 = jnp.bfloat16
F32 = jnp.float32


def rms_norm(values, norm_gain):
    mean_sq = jnp.mean(values * values, axis=-1, keepdims=True)
    return values * lax.rsqrt(mean_sq + EPSILON) * norm_gain


def after(value, *earlier):
    return lax.optimization_barrier((value,) + earlier)[0]


def in_hbm(*arrays):
    return [pltpu.with_memory_space_constraint(array, pltpu.HBM) for array in arrays]


def load_body(count, *refs):
    sources = refs[:count + 1]
    targets, bias = refs[count + 1:2 * count + 1], refs[2 * count + 1]
    table, sems = refs[2 * count + 2:]
    copies = [
        pltpu.make_async_copy(source, target, sems.at[i])
        for i, (source, target) in enumerate(zip(sources, [*targets, table]))
    ]
    for copy in copies[::-1]:
        copy.start()
    copies.pop().wait()
    heads, query_len, key_len = bias.shape
    shape = (query_len, key_len)
    offset = lax.broadcasted_iota(jnp.int32, shape, 1) - lax.broadcasted_iota(jnp.int32, shape, 0)
    bucket = jnp.clip(offset, -MAXREL, MAXREL) + MAXREL
    for h in range(heads):
        grid = jnp.full(shape, table[h, 0], F32)
        for n in range(1, NB):
            grid = jnp.where(bucket == n, table[h, n], grid)
        bias[h] = grid
    for copy in copies:
        copy.wait()


def load(weights, bias_table, query_len, key_len):
    count = len(weights)
    heads = bias_table.shape[0]
    size = sum(w.size * w.dtype.itemsize for w in weights)
    return pl.pallas_call(
        functools.partial(load_body, count),
        in_specs=[IN_HBM] * (count + 1),
        out_specs=[IN_VMEM] * (count + 1),
        out_shape=[jax.ShapeDtypeStruct(w.shape, w.dtype) for w in weights]
        + [jax.ShapeDtypeStruct((heads, query_len, key_len), F32)],
        scratch_shapes=[
            pltpu.SMEM(bias_table.shape, bias_table.dtype),
            pltpu.SemaphoreType.DMA((count + 1,)),
        ],
        compiler_params=pltpu.CompilerParams(vmem_limit_bytes=VMEM_LIMIT),
        cost_estimate=pl.CostEstimate(flops=0, bytes_accessed=2 * size, transcendentals=0),
        name="load",
    )(*in_hbm(*weights, bias_table))


def stack_body(*refs):
    sources, out, sems = refs[:-2], refs[-2], refs[-1]
    copies = [
        pltpu.make_async_copy(source, out.at[i], sems.at[i]) for i, source in enumerate(sources)
    ]
    for copy in copies:
        copy.start()
    for copy in copies:
        copy.wait()


def load_stack(weights):
    count = len(weights)
    return pl.pallas_call(
        stack_body,
        in_specs=[IN_HBM] * count,
        out_specs=IN_VMEM,
        out_shape=jax.ShapeDtypeStruct((count,) + weights[0].shape, weights[0].dtype),
        scratch_shapes=[pltpu.SemaphoreType.DMA((count,))],
        compiler_params=pltpu.CompilerParams(vmem_limit_bytes=VMEM_LIMIT),
        name="load_stack",
    )(*in_hbm(*weights))


def dot(a, b):
    return jnp.dot(a, b, preferred_element_type=F32)


def softmax_contexts(query, key, value, bias, masks):
    parts = len(masks)
    query_len, key_len = query.shape[0] // parts, key.shape[0] // parts
    ones = jnp.ones((key_len, HD), BF16)
    units = [(i, h) for i in range(parts) for h in range(query.shape[1] // HD)]

    def take(rows, length, unit):
        i, h = unit
        return rows[i * length:(i + 1) * length, h * HD:(h + 1) * HD]

    scores = [
        lax.dot_general(
            take(query, query_len, unit), take(key, key_len, unit), (((1,), (1,)), ((), ())),
            preferred_element_type=F32,
        )
        for unit in units
    ]
    scores = [score * HD ** (-0.5) for score in scores]
    if bias is not None:
        scores = [score + bias[h] for (_, h), score in zip(units, scores)]
    scores = [jnp.where(masks[i], score, NEG_FILL) for (i, _), score in zip(units, scores)]
    row_max = [jnp.max(score, axis=-1, keepdims=True) for score in scores]
    exponent = [jnp.exp(score - top).astype(BF16) for score, top in zip(scores, row_max)]
    summed = [
        dot(part, jnp.concatenate([take(value, key_len, unit), ones], axis=1))
        for unit, part in zip(units, exponent)
    ]
    context = [(total[:, :HD] / total[:, HD:]).astype(BF16) for total in summed]
    heads = len(units) // parts
    return jnp.concatenate(
        [jnp.concatenate(context[i * heads:(i + 1) * heads], axis=1) for i in range(parts)], axis=0
    )


def self_body(parts, first_slot, size, *refs):
    lengths, rows_in, weights = refs[0], refs[1:1 + parts], refs[1 + parts:5 + parts]
    bias, gain, outs = refs[5 + parts], refs[6 + parts], refs[7 + parts:]
    rows = jnp.concatenate([ref[...] for ref in rows_in], axis=0)
    rows = rms_norm(rows.astype(F32), gain[...]).astype(BF16)
    length = rows_in[0].shape[0]
    first = lax.axis_index("dp") * size
    here = lax.axis_index("tensor")
    key_index = lax.broadcasted_iota(jnp.int32, (length, length), 1)
    masks = [key_index < lengths[first + (here ^ (first_slot + i))] for i in range(parts)]
    queries, keys, values = [dot(rows, weights[i][...]).astype(BF16) for i in range(3)]
    context = softmax_contexts(queries, keys, values, bias, masks)
    term = dot(context, weights[3][...]).astype(BF16)
    for i in range(parts):
        outs[i][...] = term[i * length:(i + 1) * length]


def self_attention(lengths, first_slot, rows, weights, bias, gain):
    parts = len(rows)
    length, width = rows[0].shape
    columns = weights[0].shape[1]
    operands = [*rows, *weights, bias, gain]
    return pl.pallas_call(
        functools.partial(self_body, parts, first_slot, lax.axis_size("tensor")),
        in_specs=[IN_SMEM] + [IN_VMEM] * len(operands),
        out_specs=[IN_VMEM] * parts,
        out_shape=[jax.ShapeDtypeStruct((length, width), BF16)] * parts,
        compiler_params=pltpu.CompilerParams(vmem_limit_bytes=VMEM_LIMIT),
        cost_estimate=pl.CostEstimate(
            flops=parts * length * columns * (8 * width + 4 * length),
            bytes_accessed=4 * parts * length * width,
            transcendentals=0,
        ),
        name="self_attention",
    )(lengths, *operands)


def cross_body(slot, size, stacks, lengths, keys_in, queries_in, *refs):
    own = [ref.at[i] for ref in refs[:stacks] for i in range(ref.shape[0])]
    other = [ref.at[i] for ref in refs[stacks:2 * stacks] for i in range(ref.shape[0])]
    out = refs[-1]
    length = lengths[lax.axis_index("dp") * size + (lax.axis_index("tensor") ^ slot)]
    shape = (queries_in.shape[0], keys_in.shape[0])
    mask = lax.broadcasted_iota(jnp.int32, shape, 1) < length

    def project(rows, which):
        parts = [dot(rows[...], weights[which][...]) for weights in (own, other)]
        return jnp.concatenate(parts, axis=1).astype(BF16)

    queries, keys, values = project(queries_in, 0), project(keys_in, 1), project(keys_in, 2)
    context = softmax_contexts(queries, keys, values, None, [mask])
    half = context.shape[1] // 2
    term = dot(context[:, :half], own[3][...]) + dot(context[:, half:], other[3][...])
    out[...] = term.astype(BF16)


def cross_attention(lengths, slot, key_rows, query_rows, own, other):
    key_len, width = key_rows.shape
    query_len = query_rows.shape[0]
    columns = own[0].shape[2] * 2
    return pl.pallas_call(
        functools.partial(cross_body, slot, lax.axis_size("tensor"), len(own)),
        in_specs=[IN_SMEM] + [IN_VMEM] * (2 + 2 * len(own)),
        out_specs=IN_VMEM,
        out_shape=jax.ShapeDtypeStruct((query_len, width), BF16),
        compiler_params=pltpu.CompilerParams(vmem_limit_bytes=VMEM_LIMIT),
        cost_estimate=pl.CostEstimate(
            flops=4 * columns * (width * (query_len + key_len) + query_len * key_len),
            bytes_accessed=4 * width * (query_len + key_len),
            transcendentals=0,
        ),
        name="cross_attention",
    )(lengths, key_rows, query_rows, *own, *other)


def ffn_body(parts, *refs):
    row_parts = refs[:parts]
    w_in, w_out = refs[parts:parts + 2]
    outs = refs[parts + 2:2 * parts + 2]
    (activated,) = refs[2 * parts + 2:]
    part_len = row_parts[0].shape[0]
    rows = jnp.concatenate([ref[...] for ref in row_parts], axis=0)
    block = min(FFN_STEP, w_in.shape[1])
    for start in range(0, w_in.shape[1], block):
        cols = slice(start, start + block)
        activated[:, cols] = jnp.maximum(dot(rows, w_in[:, cols]), 0.0).astype(BF16)
    block = min(OUT_STEP, w_out.shape[1])
    for start in range(0, w_out.shape[1], block):
        cols = slice(start, start + block)
        term = dot(activated[...], w_out[:, cols]).astype(BF16)
        for i in range(parts):
            outs[i][:, cols] = term[i * part_len:(i + 1) * part_len]


def ffn(row_parts, w_in, w_out):
    parts = len(row_parts)
    part_len, width = row_parts[0].shape
    hidden = w_in.shape[1]
    rows = parts * part_len
    return pl.pallas_call(
        functools.partial(ffn_body, parts),
        in_specs=[IN_VMEM] * (parts + 2),
        out_specs=[IN_VMEM] * parts,
        out_shape=[jax.ShapeDtypeStruct((part_len, width), BF16)] * parts,
        scratch_shapes=[pltpu.VMEM((rows, hidden), BF16)],
        compiler_params=pltpu.CompilerParams(vmem_limit_bytes=VMEM_LIMIT),
        cost_estimate=pl.CostEstimate(
            flops=4 * rows * width * hidden,
            bytes_accessed=4 * rows * width,
            transcendentals=0,
        ),
        name="feed_forward",
    )(*row_parts, w_in, w_out)


def swap(value, bits):
    size = lax.axis_size("tensor")
    return lax.ppermute(value, "tensor", [(i, i ^ bits) for i in range(size)])


def spread(block):
    size = lax.axis_size("tensor")
    slots = {0: block}
    bit = size // 2
    while bit > 1:
        for k in sorted(slots):
            slots[k ^ bit] = swap(slots[k], bit)
        bit //= 2
    return [slots[2 * k] for k in range(size // 2)]


def bf16_sum(*terms):
    total = terms[0].astype(F32)
    for term in terms[1:]:
        total = total + term.astype(F32)
    return total.astype(BF16)


def pair_order(name, last):
    if OPT[name] == "213":
        return [*range(2, last, 2), *range(1, last + 1, 2)]
    return list(range(1, last + 1))


def exchange(name, block, run, both, hook=None, done=None, straight=False):
    size = lax.axis_size("tensor")
    last = size // 2 - 1
    before, late = {}, []
    order = pair_order(name, last)

    def work(k, rows, other_rows):
        if not both:
            return [run(k, rows)]
        own, other = run(k, [rows, other_rows])
        return [own, swap(other, 1)]

    block_other = swap(block, 1) if both else block
    addends = work(0, block, block_other)
    if hook is not None:
        before, late = hook(addends[0])
    slots = {0: block}
    bit = size // 2
    while bit > 1:
        for k in sorted(slots):
            slots[k ^ bit] = swap(slots[k], bit)
        bit //= 2
        if bit > 1 and name in OPT["p3tie"]:
            for k in sorted(slots):
                if k:
                    slots[k] = after(slots[k], addends[0])
    near, held, far = {}, [addends[0]], {}
    for k in order:
        held += before.get(k, [])
        if k == 1 and name in OPT["p3"]:
            held.append(slots[2 * last])
        ready = after(slots[2 * k], *held)
        other = ready if k == last else slots[2 * k]
        terms = work(k, ready, swap(other, 1) if both else None)
        held = [terms[0]]
        if k in near:
            terms.append(near[k])
        if k == last and late:
            terms[0] = after(terms[0], *late)
        partial_sum = bf16_sum(*terms) if len(terms) > 1 else terms[0]
        if done is not None:
            done[k] = partial_sum
        if k % 2 == 0:
            near[k + 1] = swap(partial_sum, 2)
        elif k == 1 or not straight:
            addends.append(swap(partial_sum, 2 * k))
        else:
            far[k] = partial_sum
    return (addends, far) if straight else addends


def decoder_body(tags, dec_rows, table, sent, *scratch):
    langs, sems = scratch
    copies = [
        pltpu.make_async_copy(dec_rows, sent.at[:dec_rows.shape[0]], sems.at[0]),
        pltpu.make_async_copy(table, langs, sems.at[1]),
    ]
    for copy in copies:
        copy.start()
    for copy in copies:
        copy.wait()
    count = dec_rows.shape[0]
    tag = tags[lax.axis_index("tensor")]
    chosen = lax.broadcasted_iota(jnp.int32, langs.shape, 0) == tag
    row = jnp.sum(jnp.where(chosen, langs[...].astype(F32), 0.0), axis=0, keepdims=True)
    shape = (sent.shape[0] - count, langs.shape[1])
    sent[count:, :] = jnp.broadcast_to(row, shape).astype(BF16)


def decoder_rows(dec_rows, table, tags):
    count, width = dec_rows.shape
    return pl.pallas_call(
        decoder_body,
        in_specs=[IN_SMEM] + [IN_HBM] * 2,
        out_specs=IN_VMEM,
        out_shape=jax.ShapeDtypeStruct((count + LANG_ROWS, width), BF16),
        scratch_shapes=[
            pltpu.VMEM(table.shape, table.dtype),
            pltpu.SemaphoreType.DMA((2,)),
        ],
        compiler_params=pltpu.CompilerParams(vmem_limit_bytes=VMEM_LIMIT),
        name="decoder_rows",
    )(tags, *in_hbm(dec_rows, table))


def norm_body(count, copies, *refs):
    addends = refs[:count]
    gain = refs[count]
    outs = refs[count + 1:]
    total = addends[0][...].astype(F32)
    for ref in addends[1:]:
        total = total + ref[...].astype(F32)
    normed = rms_norm(total, gain[...]).astype(BF16)
    for ref in outs[:copies]:
        ref[...] = normed
    for ref in outs[copies:]:
        ref[...] = total


def norm_sum(addends, gain, copies, with_sum):
    rows, width = addends[0].shape
    out_shape = [jax.ShapeDtypeStruct((rows, width), BF16)] * copies
    if with_sum:
        out_shape.append(jax.ShapeDtypeStruct((rows, width), F32))
    return pl.pallas_call(
        functools.partial(norm_body, len(addends), copies),
        out_shape=out_shape,
        compiler_params=pltpu.CompilerParams(vmem_limit_bytes=VMEM_LIMIT),
        cost_estimate=pl.CostEstimate(
            flops=8 * rows * width,
            bytes_accessed=2 * rows * width * (len(addends) + 3),
            transcendentals=rows,
        ),
        name="sum_norm",
    )(*addends, gain[None, :])


def masked_body(count, *refs):
    ends, addends, out = refs[0], refs[1:count + 1], refs[count + 1]
    total = addends[0][...].astype(F32)
    for ref in addends[1:]:
        total = total + ref[...].astype(F32)
    keep = lax.broadcasted_iota(jnp.int32, total.shape, 0) < ends[0]
    out[...] = jnp.where(keep, total, 0.0).astype(BF16)


def masked_sum(addends, ends):
    rows, width = addends[0].shape
    return pl.pallas_call(
        functools.partial(masked_body, len(addends)),
        in_specs=[IN_SMEM] + [IN_VMEM] * len(addends),
        out_specs=IN_VMEM,
        out_shape=jax.ShapeDtypeStruct((rows, width), BF16),
        compiler_params=pltpu.CompilerParams(vmem_limit_bytes=VMEM_LIMIT),
        name="masked_sum",
    )(ends, *addends)


def on_device(
    enc_tokens,
    src_lengths,
    enc_gain,
    enc_query,
    enc_key,
    enc_value,
    enc_output,
    enc_bias,
    mem_gain,
    dec_tokens,
    tgt_lengths,
    lang_tags,
    lang_table,
    cross_gain,
    cross_query,
    cross_key,
    cross_value,
    cross_output,
    ffn_gain,
    ffn_in,
    ffn_out,
):
    groups = lax.axis_size("dp")
    size = lax.axis_size("tensor")
    per_pair = size // groups
    src_len = enc_tokens.shape[1]
    target_len = dec_tokens.shape[1]

    to_source = []
    for row in range(groups * size):
        j, m = row // size, row % size
        to_source.append((row, (m // per_pair) * size + (m % per_pair) * groups + j))
    to_home = [(b, a) for a, b in to_source]

    *enc_weights, bias = load(
        [enc_query, enc_key, enc_value, enc_output], enc_bias, src_len, src_len
    )
    sent = decoder_rows(dec_tokens[0], lang_table, lang_tags)
    if OPT["home"] != "free":
        sent = after(sent, enc_weights[0])
    arrived = lax.ppermute(sent, ("dp", "tensor"), to_source)
    dec_rows = arrived[:target_len]
    dec_lang = jnp.broadcast_to(arrived[target_len:target_len + 1], dec_rows.shape)
    dec_normed, dec_input = norm_sum([dec_rows, dec_lang], cross_gain, 1, True)
    def enc_run(k, rows):
        return self_attention(src_lengths, 2 * k, rows, enc_weights, bias, enc_gain[None, :])

    dec_slots, done = [], {}
    stacks = [[cross_query, cross_key, cross_value, cross_output]]
    if cross_query.shape != cross_output.shape:
        stacks = [stacks[0][:3], stacks[0][3:]]
    cross_own = [load_stack(weights) for weights in stacks]

    def hook(out):
        rows = after(dec_normed, out) if OPT["dtie"] else dec_normed
        dec_slots.extend(spread(rows))
        wanted = [dec_slots[1], dec_slots[size // 4]]
        before = {2: [dec_normed]} if OPT["norm2"] else {}
        late = []
        before[OPT["ls"]] = before.get(OPT["ls"], []) + cross_own
        if OPT["dec"] == "early":
            before[1] = before.get(1, []) + wanted[:1]
            before[size // 2 - 1] = before.get(size // 2 - 1, []) + wanted[1:]
        elif OPT["dec"] == "last":
            before[size // 2 - 1] = before.get(size // 2 - 1, []) + wanted
        elif OPT["dec"] == "late":
            late = wanted
        return before, late

    enc_terms = exchange("enc", enc_tokens[0], enc_run, True, hook, done)
    memory_out, enc_memory = norm_sum([enc_tokens[0]] + enc_terms, mem_gain, 2, False)

    last_sums = [*done.values(), enc_terms[1]] if OPT["w"] == "all" else [*done.values()]
    if OPT["w"] == "got":
        last_sums.append(enc_terms[2])
    cross_other = [swap(after(stack, *last_sums), 1) for stack in cross_own]

    def cross_run(k, rows):
        return cross_attention(src_lengths, 2 * k, rows, dec_slots[k], cross_own, cross_other)

    cross_terms = exchange("mem", enc_memory, cross_run, False)
    ffn_normed, hidden = norm_sum([dec_input] + cross_terms, ffn_gain, 1, True)

    def ffn_pair(k, blocks):
        return ffn(blocks, ffn_in, ffn_out)

    ffn_terms = exchange("ffn", ffn_normed, ffn_pair, True, straight=OPT["straight"])

    far_terms = {}
    if OPT["straight"]:
        ffn_terms, far_terms = ffn_terms
    home = dict(to_home)
    arrivals = [lax.ppermute(bf16_sum(hidden, *ffn_terms), ("dp", "tensor"), to_home)]
    for k, term in far_terms.items():
        way = [(d, home[d ^ (2 * k)]) for d in range(groups * size)]
        arrivals.append(lax.ppermute(term, ("dp", "tensor"), way))
    dec_out = masked_sum(arrivals, tgt_lengths)
    return (memory_out[None], dec_out[None])


def solution(mesh):
    in_specs = (
        P(("dp", "tensor"), None, None),
        P(),
        P(),
        P(None, "tensor"),
        P(None, "tensor"),
        P(None, "tensor"),
        P("tensor", None),
        P("tensor", None),
        P(),
        P(("dp", "tensor"), None, None),
        P(("dp", "tensor")),
        P("dp"),
        P(),
        P(),
        P(None, "tensor"),
        P(None, "tensor"),
        P(None, "tensor"),
        P("tensor", None),
        P(),
        P(None, "tensor"),
        P("tensor", None),
    )
    out_specs = (P(("dp", "tensor"), None, None), P(("dp", "tensor"), None, None))
    return jax.shard_map(
        on_device, mesh=mesh, in_specs=in_specs, out_specs=out_specs, check_vma=False
    )
```

```python
import functools

import jax
import jax.numpy as jnp
from jax import lax
from jax.experimental import pallas as pl
from jax.experimental.pallas import tpu as pltpu
from jax.sharding import PartitionSpec as P

HD = 128
MAXREL = 16
NB = 33
LANG_ROWS = 16
OPT = dict(enc="213", mem="213", ffn="213", p3=("enc",), p1=(), dec="early", norm2=True, p3tie=("enc", "mem", "ffn"), straight=False, pieces=1, home="w", dtie=False, w="all", ls=2)
EPSILON = 1e-06
NEG_FILL = -1e30
FFN_STEP = 512
OUT_STEP = 256
VMEM_LIMIT = 16 * 1024 * 1024

IN_VMEM = pl.BlockSpec(memory_space=pltpu.VMEM)
IN_HBM = pl.BlockSpec(memory_space=pltpu.HBM)
IN_SMEM = pl.BlockSpec(memory_space=pltpu.SMEM)
BF16 = jnp.bfloat16
F32 = jnp.float32


def rms_norm(values, norm_gain):
    mean_sq = jnp.mean(values * values, axis=-1, keepdims=True)
    return values * lax.rsqrt(mean_sq + EPSILON) * norm_gain


def after(value, *earlier):
    return lax.optimization_barrier((value,) + earlier)[0]


def in_hbm(*arrays):
    return [pltpu.with_memory_space_constraint(array, pltpu.HBM) for array in arrays]


def load_body(count, *refs):
    sources = refs[:count + 1]
    targets, bias = refs[count + 1:2 * count + 1], refs[2 * count + 1]
    table, sems = refs[2 * count + 2:]
    copies = [
        pltpu.make_async_copy(source, target, sems.at[i])
        for i, (source, target) in enumerate(zip(sources, [*targets, table]))
    ]
    for copy in copies[::-1]:
        copy.start()
    copies.pop().wait()
    heads, query_len, key_len = bias.shape
    shape = (query_len, key_len)
    offset = lax.broadcasted_iota(jnp.int32, shape, 1) - lax.broadcasted_iota(jnp.int32, shape, 0)
    bucket = jnp.clip(offset, -MAXREL, MAXREL) + MAXREL
    for h in range(heads):
        grid = jnp.full(shape, table[h, 0], F32)
        for n in range(1, NB):
            grid = jnp.where(bucket == n, table[h, n], grid)
        bias[h] = grid
    for copy in copies:
        copy.wait()


def load(weights, bias_table, query_len, key_len):
    count = len(weights)
    heads = bias_table.shape[0]
    size = sum(w.size * w.dtype.itemsize for w in weights)
    return pl.pallas_call(
        functools.partial(load_body, count),
        in_specs=[IN_HBM] * (count + 1),
        out_specs=[IN_VMEM] * (count + 1),
        out_shape=[jax.ShapeDtypeStruct(w.shape, w.dtype) for w in weights]
        + [jax.ShapeDtypeStruct((heads, query_len, key_len), F32)],
        scratch_shapes=[
            pltpu.SMEM(bias_table.shape, bias_table.dtype),
            pltpu.SemaphoreType.DMA((count + 1,)),
        ],
        compiler_params=pltpu.CompilerParams(vmem_limit_bytes=VMEM_LIMIT),
        cost_estimate=pl.CostEstimate(flops=0, bytes_accessed=2 * size, transcendentals=0),
        name="load",
    )(*in_hbm(*weights, bias_table))


def stack_body(*refs):
    sources, out, sems = refs[:-2], refs[-2], refs[-1]
    copies = [
        pltpu.make_async_copy(source, out.at[i], sems.at[i]) for i, source in enumerate(sources)
    ]
    for copy in copies:
        copy.start()
    for copy in copies:
        copy.wait()


def load_stack(weights):
    count = len(weights)
    return pl.pallas_call(
        stack_body,
        in_specs=[IN_HBM] * count,
        out_specs=IN_VMEM,
        out_shape=jax.ShapeDtypeStruct((count,) + weights[0].shape, weights[0].dtype),
        scratch_shapes=[pltpu.SemaphoreType.DMA((count,))],
        compiler_params=pltpu.CompilerParams(vmem_limit_bytes=VMEM_LIMIT),
        name="load_stack",
    )(*in_hbm(*weights))


def dot(a, b):
    return jnp.dot(a, b, preferred_element_type=F32)


def softmax_contexts(query, key, value, bias, masks):
    parts = len(masks)
    query_len, key_len = query.shape[0] // parts, key.shape[0] // parts
    ones = jnp.ones((key_len, HD), BF16)
    units = [(i, h) for i in range(parts) for h in range(query.shape[1] // HD)]

    def take(rows, length, unit):
        i, h = unit
        return rows[i * length:(i + 1) * length, h * HD:(h + 1) * HD]

    scores = [
        lax.dot_general(
            take(query, query_len, unit), take(key, key_len, unit), (((1,), (1,)), ((), ())),
            preferred_element_type=F32,
        )
        for unit in units
    ]
    scores = [score * HD ** (-0.5) for score in scores]
    if bias is not None:
        scores = [score + bias[h] for (_, h), score in zip(units, scores)]
    scores = [jnp.where(masks[i], score, NEG_FILL) for (i, _), score in zip(units, scores)]
    row_max = [jnp.max(score, axis=-1, keepdims=True) for score in scores]
    exponent = [jnp.exp(score - top).astype(BF16) for score, top in zip(scores, row_max)]
    summed = [
        dot(part, jnp.concatenate([take(value, key_len, unit), ones], axis=1))
        for unit, part in zip(units, exponent)
    ]
    context = [(total[:, :HD] / total[:, HD:]).astype(BF16) for total in summed]
    heads = len(units) // parts
    return jnp.concatenate(
        [jnp.concatenate(context[i * heads:(i + 1) * heads], axis=1) for i in range(parts)], axis=0
    )


def self_body(parts, first_slot, size, *refs):
    lengths, rows_in, weights = refs[0], refs[1:1 + parts], refs[1 + parts:5 + parts]
    bias, gain, outs = refs[5 + parts], refs[6 + parts], refs[7 + parts:]
    rows = jnp.concatenate([ref[...] for ref in rows_in], axis=0)
    rows = rms_norm(rows.astype(F32), gain[...]).astype(BF16)
    length = rows_in[0].shape[0]
    first = lax.axis_index("dp") * size
    here = lax.axis_index("tensor")
    key_index = lax.broadcasted_iota(jnp.int32, (length, length), 1)
    masks = [key_index < lengths[first + (here ^ (first_slot + i))] for i in range(parts)]
    queries, keys, values = [dot(rows, weights[i][...]).astype(BF16) for i in range(3)]
    context = softmax_contexts(queries, keys, values, bias, masks)
    term = dot(context, weights[3][...]).astype(BF16)
    for i in range(parts):
        outs[i][...] = term[i * length:(i + 1) * length]


def self_attention(lengths, first_slot, rows, weights, bias, gain):
    parts = len(rows)
    length, width = rows[0].shape
    columns = weights[0].shape[1]
    operands = [*rows, *weights, bias, gain]
    return pl.pallas_call(
        functools.partial(self_body, parts, first_slot, lax.axis_size("tensor")),
        in_specs=[IN_SMEM] + [IN_VMEM] * len(operands),
        out_specs=[IN_VMEM] * parts,
        out_shape=[jax.ShapeDtypeStruct((length, width), BF16)] * parts,
        compiler_params=pltpu.CompilerParams(vmem_limit_bytes=VMEM_LIMIT),
        cost_estimate=pl.CostEstimate(
            flops=parts * length * columns * (8 * width + 4 * length),
            bytes_accessed=4 * parts * length * width,
            transcendentals=0,
        ),
        name="self_attention",
    )(lengths, *operands)


def cross_body(slot, size, stacks, lengths, keys_in, queries_in, *refs):
    own = [ref.at[i] for ref in refs[:stacks] for i in range(ref.shape[0])]
    other = [ref.at[i] for ref in refs[stacks:2 * stacks] for i in range(ref.shape[0])]
    out = refs[-1]
    length = lengths[lax.axis_index("dp") * size + (lax.axis_index("tensor") ^ slot)]
    shape = (queries_in.shape[0], keys_in.shape[0])
    mask = lax.broadcasted_iota(jnp.int32, shape, 1) < length

    def project(rows, which):
        parts = [dot(rows[...], weights[which][...]) for weights in (own, other)]
        return jnp.concatenate(parts, axis=1).astype(BF16)

    queries, keys, values = project(queries_in, 0), project(keys_in, 1), project(keys_in, 2)
    context = softmax_contexts(queries, keys, values, None, [mask])
    half = context.shape[1] // 2
    term = dot(context[:, :half], own[3][...]) + dot(context[:, half:], other[3][...])
    out[...] = term.astype(BF16)


def cross_attention(lengths, slot, key_rows, query_rows, own, other):
    key_len, width = key_rows.shape
    query_len = query_rows.shape[0]
    columns = own[0].shape[2] * 2
    return pl.pallas_call(
        functools.partial(cross_body, slot, lax.axis_size("tensor"), len(own)),
        in_specs=[IN_SMEM] + [IN_VMEM] * (2 + 2 * len(own)),
        out_specs=IN_VMEM,
        out_shape=jax.ShapeDtypeStruct((query_len, width), BF16),
        compiler_params=pltpu.CompilerParams(vmem_limit_bytes=VMEM_LIMIT),
        cost_estimate=pl.CostEstimate(
            flops=4 * columns * (width * (query_len + key_len) + query_len * key_len),
            bytes_accessed=4 * width * (query_len + key_len),
            transcendentals=0,
        ),
        name="cross_attention",
    )(lengths, key_rows, query_rows, *own, *other)


def ffn_body(parts, *refs):
    row_parts = refs[:parts]
    w_in, w_out = refs[parts:parts + 2]
    outs = refs[parts + 2:2 * parts + 2]
    (activated,) = refs[2 * parts + 2:]
    part_len = row_parts[0].shape[0]
    rows = jnp.concatenate([ref[...] for ref in row_parts], axis=0)
    block = min(FFN_STEP, w_in.shape[1])
    for start in range(0, w_in.shape[1], block):
        cols = slice(start, start + block)
        activated[:, cols] = jnp.maximum(dot(rows, w_in[:, cols]), 0.0).astype(BF16)
    block = min(OUT_STEP, w_out.shape[1])
    for start in range(0, w_out.shape[1], block):
        cols = slice(start, start + block)
        term = dot(activated[...], w_out[:, cols]).astype(BF16)
        for i in range(parts):
            outs[i][:, cols] = term[i * part_len:(i + 1) * part_len]


def ffn(row_parts, w_in, w_out):
    parts = len(row_parts)
    part_len, width = row_parts[0].shape
    hidden = w_in.shape[1]
    rows = parts * part_len
    return pl.pallas_call(
        functools.partial(ffn_body, parts),
        in_specs=[IN_VMEM] * (parts + 2),
        out_specs=[IN_VMEM] * parts,
        out_shape=[jax.ShapeDtypeStruct((part_len, width), BF16)] * parts,
        scratch_shapes=[pltpu.VMEM((rows, hidden), BF16)],
        compiler_params=pltpu.CompilerParams(vmem_limit_bytes=VMEM_LIMIT),
        cost_estimate=pl.CostEstimate(
            flops=4 * rows * width * hidden,
            bytes_accessed=4 * rows * width,
            transcendentals=0,
        ),
        name="feed_forward",
    )(*row_parts, w_in, w_out)


def swap(value, bits):
    size = lax.axis_size("tensor")
    return lax.ppermute(value, "tensor", [(i, i ^ bits) for i in range(size)])


def spread(block):
    size = lax.axis_size("tensor")
    slots = {0: block}
    bit = size // 2
    while bit > 1:
        for k in sorted(slots):
            slots[k ^ bit] = swap(slots[k], bit)
        bit //= 2
    return [slots[2 * k] for k in range(size // 2)]


def bf16_sum(*terms):
    total = terms[0].astype(F32)
    for term in terms[1:]:
        total = total + term.astype(F32)
    return total.astype(BF16)


def pair_order(name, last):
    if OPT[name] == "213":
        return [*range(2, last, 2), *range(1, last + 1, 2)]
    return list(range(1, last + 1))


def exchange(name, block, run, both, hook=None, done=None, straight=False):
    size = lax.axis_size("tensor")
    last = size // 2 - 1
    before, late = {}, []
    order = pair_order(name, last)

    def work(k, rows, other_rows):
        if not both:
            return [run(k, rows)]
        own, other = run(k, [rows, other_rows])
        return [own, swap(other, 1)]

    block_other = swap(block, 1) if both else block
    addends = work(0, block, block_other)
    if hook is not None:
        before, late = hook(addends[0])
    slots = {0: block}
    bit = size // 2
    while bit > 1:
        for k in sorted(slots):
            slots[k ^ bit] = swap(slots[k], bit)
        bit //= 2
        if bit > 1 and name in OPT["p3tie"]:
            for k in sorted(slots):
                if k:
                    slots[k] = after(slots[k], addends[0])
    near, held, far = {}, [addends[0]], {}
    for k in order:
        held += before.get(k, [])
        if k == 1 and name in OPT["p3"]:
            held.append(slots[2 * last])
        ready = after(slots[2 * k], *held)
        other = ready if k == last else slots[2 * k]
        terms = work(k, ready, swap(other, 1) if both else None)
        held = [terms[0]]
        if k in near:
            terms.append(near[k])
        if k == last and late:
            terms[0] = after(terms[0], *late)
        partial_sum = bf16_sum(*terms) if len(terms) > 1 else terms[0]
        if done is not None:
            done[k] = partial_sum
        if k % 2 == 0:
            near[k + 1] = swap(partial_sum, 2)
        elif k == 1 or not straight:
            addends.append(swap(partial_sum, 2 * k))
        else:
            far[k] = partial_sum
    return (addends, far) if straight else addends


def decoder_body(tags, dec_rows, table, sent, *scratch):
    langs, sems = scratch
    copies = [
        pltpu.make_async_copy(dec_rows, sent.at[:dec_rows.shape[0]], sems.at[0]),
        pltpu.make_async_copy(table, langs, sems.at[1]),
    ]
    for copy in copies:
        copy.start()
    for copy in copies:
        copy.wait()
    count = dec_rows.shape[0]
    tag = tags[lax.axis_index("tensor")]
    chosen = lax.broadcasted_iota(jnp.int32, langs.shape, 0) == tag
    row = jnp.sum(jnp.where(chosen, langs[...].astype(F32), 0.0), axis=0, keepdims=True)
    shape = (sent.shape[0] - count, langs.shape[1])
    sent[count:, :] = jnp.broadcast_to(row, shape).astype(BF16)


def decoder_rows(dec_rows, table, tags):
    count, width = dec_rows.shape
    return pl.pallas_call(
        decoder_body,
        in_specs=[IN_SMEM] + [IN_HBM] * 2,
        out_specs=IN_VMEM,
        out_shape=jax.ShapeDtypeStruct((count + LANG_ROWS, width), BF16),
        scratch_shapes=[
            pltpu.VMEM(table.shape, table.dtype),
            pltpu.SemaphoreType.DMA((2,)),
        ],
        compiler_params=pltpu.CompilerParams(vmem_limit_bytes=VMEM_LIMIT),
        name="decoder_rows",
    )(tags, *in_hbm(dec_rows, table))


def norm_body(count, copies, *refs):
    addends = refs[:count]
    gain = refs[count]
    outs = refs[count + 1:]
    total = addends[0][...].astype(F32)
    for ref in addends[1:]:
        total = total + ref[...].astype(F32)
    normed = rms_norm(total, gain[...]).astype(BF16)
    for ref in outs[:copies]:
        ref[...] = normed
    for ref in outs[copies:]:
        ref[...] = total


def norm_sum(addends, gain, copies, with_sum):
    rows, width = addends[0].shape
    out_shape = [jax.ShapeDtypeStruct((rows, width), BF16)] * copies
    if with_sum:
        out_shape.append(jax.ShapeDtypeStruct((rows, width), F32))
    return pl.pallas_call(
        functools.partial(norm_body, len(addends), copies),
        out_shape=out_shape,
        compiler_params=pltpu.CompilerParams(vmem_limit_bytes=VMEM_LIMIT),
        cost_estimate=pl.CostEstimate(
            flops=8 * rows * width,
            bytes_accessed=2 * rows * width * (len(addends) + 3),
            transcendentals=rows,
        ),
        name="sum_norm",
    )(*addends, gain[None, :])


def masked_body(ends, *refs):
    pieces, out = refs[:-1], refs[-1]
    count = pieces[0].shape[0]
    for i, ref in enumerate(pieces):
        index = lax.broadcasted_iota(jnp.int32, ref.shape, 0) + i * count
        out[i * count:(i + 1) * count, :] = jnp.where(
            index < ends[0], ref[...].astype(F32), 0.0
        ).astype(BF16)


def masked(pieces, ends):
    rows, width = pieces[0].shape
    return pl.pallas_call(
        masked_body,
        in_specs=[IN_SMEM] + [IN_VMEM] * len(pieces),
        out_specs=IN_VMEM,
        out_shape=jax.ShapeDtypeStruct((rows * len(pieces), width), BF16),
        compiler_params=pltpu.CompilerParams(vmem_limit_bytes=VMEM_LIMIT),
        name="masked",
    )(ends, *pieces)


def on_device(
    enc_tokens,
    src_lengths,
    enc_gain,
    enc_query,
    enc_key,
    enc_value,
    enc_output,
    enc_bias,
    mem_gain,
    dec_tokens,
    tgt_lengths,
    lang_tags,
    lang_table,
    cross_gain,
    cross_query,
    cross_key,
    cross_value,
    cross_output,
    ffn_gain,
    ffn_in,
    ffn_out,
):
    groups = lax.axis_size("dp")
    size = lax.axis_size("tensor")
    per_pair = size // groups
    src_len = enc_tokens.shape[1]
    target_len = dec_tokens.shape[1]

    to_source = []
    for row in range(groups * size):
        j, m = row // size, row % size
        to_source.append((row, (m // per_pair) * size + (m % per_pair) * groups + j))
    to_home = [(b, a) for a, b in to_source]

    *enc_weights, bias = load(
        [enc_query, enc_key, enc_value, enc_output], enc_bias, src_len, src_len
    )
    sent = decoder_rows(dec_tokens[0], lang_table, lang_tags)
    if OPT["home"] != "free":
        sent = after(sent, enc_weights[0])
    arrived = lax.ppermute(sent, ("dp", "tensor"), to_source)
    dec_rows = arrived[:target_len]
    dec_lang = jnp.broadcast_to(arrived[target_len:target_len + 1], dec_rows.shape)
    dec_normed, dec_input = norm_sum([dec_rows, dec_lang], cross_gain, 1, True)
    def enc_run(k, rows):
        return self_attention(src_lengths, 2 * k, rows, enc_weights, bias, enc_gain[None, :])

    dec_slots, done = [], {}
    stacks = [[cross_query, cross_key, cross_value, cross_output]]
    if cross_query.shape != cross_output.shape:
        stacks = [stacks[0][:3], stacks[0][3:]]
    cross_own = [load_stack(weights) for weights in stacks]
    if OPT["ls"] == 0:
        enc_weights[0] = after(enc_weights[0], *cross_own)

    def hook(out):
        rows = after(dec_normed, out) if OPT["dtie"] else dec_normed
        dec_slots.extend(spread(rows))
        wanted = [dec_slots[1], dec_slots[size // 4]]
        before = {2: [dec_normed]} if OPT["norm2"] else {}
        late = []
        before[OPT["ls"]] = before.get(OPT["ls"], []) + cross_own
        if OPT["dec"] == "early":
            before[1] = before.get(1, []) + wanted[:1]
            before[size // 2 - 1] = before.get(size // 2 - 1, []) + wanted[1:]
        elif OPT["dec"] == "last":
            before[size // 2 - 1] = before.get(size // 2 - 1, []) + wanted
        elif OPT["dec"] == "late":
            late = wanted
        return before, late

    enc_terms = exchange("enc", enc_tokens[0], enc_run, True, hook, done)
    memory_out, enc_memory = norm_sum([enc_tokens[0]] + enc_terms, mem_gain, 2, False)

    last_sums = [*done.values(), enc_terms[1]] if OPT["w"] == "all" else [*done.values()]
    if OPT["w"] == "got":
        last_sums.append(enc_terms[2])
    cross_other = [swap(after(stack, *last_sums), 1) for stack in cross_own]

    def cross_run(k, rows):
        return cross_attention(src_lengths, 2 * k, rows, dec_slots[k], cross_own, cross_other)

    cross_terms = exchange("mem", enc_memory, cross_run, False)
    ffn_normed, hidden = norm_sum([dec_input] + cross_terms, ffn_gain, 1, True)

    def ffn_pair(k, blocks):
        return ffn(blocks, ffn_in, ffn_out)

    ffn_terms = exchange("ffn", ffn_normed, ffn_pair, True, straight=OPT["straight"])

    if OPT["straight"]:
        ffn_terms, far_terms = ffn_terms
        pieces = []
        step = target_len // OPT["pieces"]
        for start in range(0, target_len, step):
            rows = slice(start, start + step)
            terms = [term[rows] for term in (hidden, *ffn_terms)]
            terms += [swap(term[rows], 2 * k) for k, term in far_terms.items()]
            pieces.append(lax.ppermute(bf16_sum(*terms), ("dp", "tensor"), to_home))
    else:
        pieces = [lax.ppermute(bf16_sum(hidden, *ffn_terms), ("dp", "tensor"), to_home)]
    dec_out = masked(pieces, tgt_lengths)
    return (memory_out[None], dec_out[None])


def solution(mesh):
    in_specs = (
        P(("dp", "tensor"), None, None),
        P(),
        P(),
        P(None, "tensor"),
        P(None, "tensor"),
        P(None, "tensor"),
        P("tensor", None),
        P("tensor", None),
        P(),
        P(("dp", "tensor"), None, None),
        P(("dp", "tensor")),
        P("dp"),
        P(),
        P(),
        P(None, "tensor"),
        P(None, "tensor"),
        P(None, "tensor"),
        P("tensor", None),
        P(),
        P(None, "tensor"),
        P("tensor", None),
    )
    out_specs = (P(("dp", "tensor"), None, None), P(("dp", "tensor"), None, None))
    return jax.shard_map(
        on_device, mesh=mesh, in_specs=in_specs, out_specs=out_specs, check_vma=False
    )
```

```python
import functools

import jax
import jax.numpy as jnp
from jax import lax
from jax.experimental import pallas as pl
from jax.experimental.pallas import tpu as pltpu
from jax.sharding import PartitionSpec as P

HD = 128
MAXREL = 16
NB = 33
LANG_ROWS = 16
OPT = dict(enc="213", mem="213", ffn="213", p3=("enc",), p1=(), dec="early", norm2=True, p3tie=("enc", "mem", "ffn"), straight=False, pieces=1, home="w", dtie=True, w="all", ls=2)
EPSILON = 1e-06
NEG_FILL = -1e30
FFN_STEP = 512
OUT_STEP = 256
VMEM_LIMIT = 10 * 1024 * 1024

IN_VMEM = pl.BlockSpec(memory_space=pltpu.VMEM)
IN_HBM = pl.BlockSpec(memory_space=pltpu.HBM)
IN_SMEM = pl.BlockSpec(memory_space=pltpu.SMEM)
BF16 = jnp.bfloat16
F32 = jnp.float32


def rms_norm(values, norm_gain):
    mean_sq = jnp.mean(values * values, axis=-1, keepdims=True)
    return values * lax.rsqrt(mean_sq + EPSILON) * norm_gain


def after(value, *earlier):
    return lax.optimization_barrier((value,) + earlier)[0]


def in_hbm(*arrays):
    return [pltpu.with_memory_space_constraint(array, pltpu.HBM) for array in arrays]


def load_body(count, *refs):
    sources = refs[:count + 1]
    targets, bias = refs[count + 1:2 * count + 1], refs[2 * count + 1]
    table, sems = refs[2 * count + 2:]
    copies = [
        pltpu.make_async_copy(source, target, sems.at[i])
        for i, (source, target) in enumerate(zip(sources, [*targets, table]))
    ]
    for copy in copies[::-1]:
        copy.start()
    copies.pop().wait()
    heads, query_len, key_len = bias.shape
    shape = (query_len, key_len)
    offset = lax.broadcasted_iota(jnp.int32, shape, 1) - lax.broadcasted_iota(jnp.int32, shape, 0)
    bucket = jnp.clip(offset, -MAXREL, MAXREL) + MAXREL
    for h in range(heads):
        grid = jnp.full(shape, table[h, 0], F32)
        for n in range(1, NB):
            grid = jnp.where(bucket == n, table[h, n], grid)
        bias[h] = grid
    for copy in copies:
        copy.wait()


def load(weights, bias_table, query_len, key_len):
    count = len(weights)
    heads = bias_table.shape[0]
    size = sum(w.size * w.dtype.itemsize for w in weights)
    return pl.pallas_call(
        functools.partial(load_body, count),
        in_specs=[IN_HBM] * (count + 1),
        out_specs=[IN_VMEM] * (count + 1),
        out_shape=[jax.ShapeDtypeStruct(w.shape, w.dtype) for w in weights]
        + [jax.ShapeDtypeStruct((heads, query_len, key_len), F32)],
        scratch_shapes=[
            pltpu.SMEM(bias_table.shape, bias_table.dtype),
            pltpu.SemaphoreType.DMA((count + 1,)),
        ],
        compiler_params=pltpu.CompilerParams(vmem_limit_bytes=VMEM_LIMIT),
        cost_estimate=pl.CostEstimate(flops=0, bytes_accessed=2 * size, transcendentals=0),
        name="load",
    )(*in_hbm(*weights, bias_table))


def stack_body(*refs):
    sources, out, sems = refs[:-2], refs[-2], refs[-1]
    copies = [
        pltpu.make_async_copy(source, out.at[i], sems.at[i]) for i, source in enumerate(sources)
    ]
    for copy in copies:
        copy.start()
    for copy in copies:
        copy.wait()


def load_stack(weights):
    count = len(weights)
    return pl.pallas_call(
        stack_body,
        in_specs=[IN_HBM] * count,
        out_specs=IN_VMEM,
        out_shape=jax.ShapeDtypeStruct((count,) + weights[0].shape, weights[0].dtype),
        scratch_shapes=[pltpu.SemaphoreType.DMA((count,))],
        compiler_params=pltpu.CompilerParams(vmem_limit_bytes=VMEM_LIMIT),
        name="load_stack",
    )(*in_hbm(*weights))


def dot(a, b):
    return jnp.dot(a, b, preferred_element_type=F32)


def softmax_contexts(query, key, value, bias, masks):
    parts = len(masks)
    query_len, key_len = query.shape[0] // parts, key.shape[0] // parts
    ones = jnp.ones((key_len, HD), BF16)
    units = [(i, h) for i in range(parts) for h in range(query.shape[1] // HD)]

    def take(rows, length, unit):
        i, h = unit
        return rows[i * length:(i + 1) * length, h * HD:(h + 1) * HD]

    scores = [
        lax.dot_general(
            take(query, query_len, unit), take(key, key_len, unit), (((1,), (1,)), ((), ())),
            preferred_element_type=F32,
        )
        for unit in units
    ]
    scores = [score * HD ** (-0.5) for score in scores]
    if bias is not None:
        scores = [score + bias[h] for (_, h), score in zip(units, scores)]
    scores = [jnp.where(masks[i], score, NEG_FILL) for (i, _), score in zip(units, scores)]
    row_max = [jnp.max(score, axis=-1, keepdims=True) for score in scores]
    exponent = [jnp.exp(score - top).astype(BF16) for score, top in zip(scores, row_max)]
    summed = [
        dot(part, jnp.concatenate([take(value, key_len, unit), ones], axis=1))
        for unit, part in zip(units, exponent)
    ]
    context = [(total[:, :HD] / total[:, HD:]).astype(BF16) for total in summed]
    heads = len(units) // parts
    return jnp.concatenate(
        [jnp.concatenate(context[i * heads:(i + 1) * heads], axis=1) for i in range(parts)], axis=0
    )


def self_body(parts, first_slot, size, *refs):
    lengths, rows_in, weights = refs[0], refs[1:1 + parts], refs[1 + parts:5 + parts]
    bias, gain, outs = refs[5 + parts], refs[6 + parts], refs[7 + parts:]
    rows = jnp.concatenate([ref[...] for ref in rows_in], axis=0)
    rows = rms_norm(rows.astype(F32), gain[...]).astype(BF16)
    length = rows_in[0].shape[0]
    first = lax.axis_index("dp") * size
    here = lax.axis_index("tensor")
    key_index = lax.broadcasted_iota(jnp.int32, (length, length), 1)
    masks = [key_index < lengths[first + (here ^ (first_slot + i))] for i in range(parts)]
    queries, keys, values = [dot(rows, weights[i][...]).astype(BF16) for i in range(3)]
    context = softmax_contexts(queries, keys, values, bias, masks)
    term = dot(context, weights[3][...]).astype(BF16)
    for i in range(parts):
        outs[i][...] = term[i * length:(i + 1) * length]


def self_attention(lengths, first_slot, rows, weights, bias, gain):
    parts = len(rows)
    length, width = rows[0].shape
    columns = weights[0].shape[1]
    operands = [*rows, *weights, bias, gain]
    return pl.pallas_call(
        functools.partial(self_body, parts, first_slot, lax.axis_size("tensor")),
        in_specs=[IN_SMEM] + [IN_VMEM] * len(operands),
        out_specs=[IN_VMEM] * parts,
        out_shape=[jax.ShapeDtypeStruct((length, width), BF16)] * parts,
        compiler_params=pltpu.CompilerParams(vmem_limit_bytes=VMEM_LIMIT),
        cost_estimate=pl.CostEstimate(
            flops=parts * length * columns * (8 * width + 4 * length),
            bytes_accessed=4 * parts * length * width,
            transcendentals=0,
        ),
        name="self_attention",
    )(lengths, *operands)


def cross_body(slot, size, stacks, lengths, keys_in, queries_in, *refs):
    own = [ref.at[i] for ref in refs[:stacks] for i in range(ref.shape[0])]
    other = [ref.at[i] for ref in refs[stacks:2 * stacks] for i in range(ref.shape[0])]
    out = refs[-1]
    length = lengths[lax.axis_index("dp") * size + (lax.axis_index("tensor") ^ slot)]
    shape = (queries_in.shape[0], keys_in.shape[0])
    mask = lax.broadcasted_iota(jnp.int32, shape, 1) < length

    def project(rows, which):
        parts = [dot(rows[...], weights[which][...]) for weights in (own, other)]
        return jnp.concatenate(parts, axis=1).astype(BF16)

    queries, keys, values = project(queries_in, 0), project(keys_in, 1), project(keys_in, 2)
    context = softmax_contexts(queries, keys, values, None, [mask])
    half = context.shape[1] // 2
    term = dot(context[:, :half], own[3][...]) + dot(context[:, half:], other[3][...])
    out[...] = term.astype(BF16)


def cross_attention(lengths, slot, key_rows, query_rows, own, other):
    key_len, width = key_rows.shape
    query_len = query_rows.shape[0]
    columns = own[0].shape[2] * 2
    return pl.pallas_call(
        functools.partial(cross_body, slot, lax.axis_size("tensor"), len(own)),
        in_specs=[IN_SMEM] + [IN_VMEM] * (2 + 2 * len(own)),
        out_specs=IN_VMEM,
        out_shape=jax.ShapeDtypeStruct((query_len, width), BF16),
        compiler_params=pltpu.CompilerParams(vmem_limit_bytes=VMEM_LIMIT),
        cost_estimate=pl.CostEstimate(
            flops=4 * columns * (width * (query_len + key_len) + query_len * key_len),
            bytes_accessed=4 * width * (query_len + key_len),
            transcendentals=0,
        ),
        name="cross_attention",
    )(lengths, key_rows, query_rows, *own, *other)


def ffn_body(parts, *refs):
    row_parts = refs[:parts]
    w_in, w_out = refs[parts:parts + 2]
    outs = refs[parts + 2:2 * parts + 2]
    (activated,) = refs[2 * parts + 2:]
    part_len = row_parts[0].shape[0]
    rows = jnp.concatenate([ref[...] for ref in row_parts], axis=0)
    block = min(FFN_STEP, w_in.shape[1])
    for start in range(0, w_in.shape[1], block):
        cols = slice(start, start + block)
        activated[:, cols] = jnp.maximum(dot(rows, w_in[:, cols]), 0.0).astype(BF16)
    block = min(OUT_STEP, w_out.shape[1])
    for start in range(0, w_out.shape[1], block):
        cols = slice(start, start + block)
        term = dot(activated[...], w_out[:, cols]).astype(BF16)
        for i in range(parts):
            outs[i][:, cols] = term[i * part_len:(i + 1) * part_len]


def ffn(row_parts, w_in, w_out):
    parts = len(row_parts)
    part_len, width = row_parts[0].shape
    hidden = w_in.shape[1]
    rows = parts * part_len
    return pl.pallas_call(
        functools.partial(ffn_body, parts),
        in_specs=[IN_VMEM] * (parts + 2),
        out_specs=[IN_VMEM] * parts,
        out_shape=[jax.ShapeDtypeStruct((part_len, width), BF16)] * parts,
        scratch_shapes=[pltpu.VMEM((rows, hidden), BF16)],
        compiler_params=pltpu.CompilerParams(vmem_limit_bytes=VMEM_LIMIT),
        cost_estimate=pl.CostEstimate(
            flops=4 * rows * width * hidden,
            bytes_accessed=4 * rows * width,
            transcendentals=0,
        ),
        name="feed_forward",
    )(*row_parts, w_in, w_out)


def swap(value, bits):
    size = lax.axis_size("tensor")
    return lax.ppermute(value, "tensor", [(i, i ^ bits) for i in range(size)])


def spread(block):
    size = lax.axis_size("tensor")
    slots = {0: block}
    bit = size // 2
    while bit > 1:
        for k in sorted(slots):
            slots[k ^ bit] = swap(slots[k], bit)
        bit //= 2
    return [slots[2 * k] for k in range(size // 2)]


def bf16_sum(*terms):
    total = terms[0].astype(F32)
    for term in terms[1:]:
        total = total + term.astype(F32)
    return total.astype(BF16)


def pair_order(name, last):
    if OPT[name] == "213":
        return [*range(2, last, 2), *range(1, last + 1, 2)]
    return list(range(1, last + 1))


def exchange(name, block, run, both, hook=None, done=None, straight=False):
    size = lax.axis_size("tensor")
    last = size // 2 - 1
    before, late = {}, []
    order = pair_order(name, last)

    def work(k, rows, other_rows):
        if not both:
            return [run(k, rows)]
        own, other = run(k, [rows, other_rows])
        return [own, swap(other, 1)]

    block_other = swap(block, 1) if both else block
    addends = work(0, block, block_other)
    if hook is not None:
        before, late = hook(addends[0])
    slots = {0: block}
    bit = size // 2
    while bit > 1:
        for k in sorted(slots):
            slots[k ^ bit] = swap(slots[k], bit)
        bit //= 2
        if bit > 1 and name in OPT["p3tie"]:
            for k in sorted(slots):
                if k:
                    slots[k] = after(slots[k], addends[0])
    near, held, far = {}, [addends[0]], {}
    for k in order:
        held += before.get(k, [])
        if k == 1 and name in OPT["p3"]:
            held.append(slots[2 * last])
        ready = after(slots[2 * k], *held)
        other = ready if k == last else slots[2 * k]
        terms = work(k, ready, swap(other, 1) if both else None)
        held = [terms[0]]
        if k in near:
            terms.append(near[k])
        if k == last and late:
            terms[0] = after(terms[0], *late)
        partial_sum = bf16_sum(*terms) if len(terms) > 1 else terms[0]
        if done is not None:
            done[k] = partial_sum
        if k % 2 == 0:
            near[k + 1] = swap(partial_sum, 2)
        elif k == 1 or not straight:
            addends.append(swap(partial_sum, 2 * k))
        else:
            far[k] = partial_sum
    return (addends, far) if straight else addends


def decoder_body(tags, dec_rows, table, sent, *scratch):
    langs, sems = scratch
    copies = [
        pltpu.make_async_copy(dec_rows, sent.at[:dec_rows.shape[0]], sems.at[0]),
        pltpu.make_async_copy(table, langs, sems.at[1]),
    ]
    for copy in copies:
        copy.start()
    for copy in copies:
        copy.wait()
    count = dec_rows.shape[0]
    tag = tags[lax.axis_index("tensor")]
    chosen = lax.broadcasted_iota(jnp.int32, langs.shape, 0) == tag
    row = jnp.sum(jnp.where(chosen, langs[...].astype(F32), 0.0), axis=0, keepdims=True)
    shape = (sent.shape[0] - count, langs.shape[1])
    sent[count:, :] = jnp.broadcast_to(row, shape).astype(BF16)


def decoder_rows(dec_rows, table, tags):
    count, width = dec_rows.shape
    return pl.pallas_call(
        decoder_body,
        in_specs=[IN_SMEM] + [IN_HBM] * 2,
        out_specs=IN_VMEM,
        out_shape=jax.ShapeDtypeStruct((count + LANG_ROWS, width), BF16),
        scratch_shapes=[
            pltpu.VMEM(table.shape, table.dtype),
            pltpu.SemaphoreType.DMA((2,)),
        ],
        compiler_params=pltpu.CompilerParams(vmem_limit_bytes=VMEM_LIMIT),
        name="decoder_rows",
    )(tags, *in_hbm(dec_rows, table))


def norm_body(count, copies, *refs):
    addends = refs[:count]
    gain = refs[count]
    outs = refs[count + 1:]
    total = addends[0][...].astype(F32)
    for ref in addends[1:]:
        total = total + ref[...].astype(F32)
    normed = rms_norm(total, gain[...]).astype(BF16)
    for ref in outs[:copies]:
        ref[...] = normed
    for ref in outs[copies:]:
        ref[...] = total


def norm_sum(addends, gain, copies, with_sum):
    rows, width = addends[0].shape
    out_shape = [jax.ShapeDtypeStruct((rows, width), BF16)] * copies
    if with_sum:
        out_shape.append(jax.ShapeDtypeStruct((rows, width), F32))
    return pl.pallas_call(
        functools.partial(norm_body, len(addends), copies),
        out_shape=out_shape,
        compiler_params=pltpu.CompilerParams(vmem_limit_bytes=VMEM_LIMIT),
        cost_estimate=pl.CostEstimate(
            flops=8 * rows * width,
            bytes_accessed=2 * rows * width * (len(addends) + 3),
            transcendentals=rows,
        ),
        name="sum_norm",
    )(*addends, gain[None, :])


def masked_body(ends, *refs):
    pieces, out = refs[:-1], refs[-1]
    count = pieces[0].shape[0]
    for i, ref in enumerate(pieces):
        index = lax.broadcasted_iota(jnp.int32, ref.shape, 0) + i * count
        out[i * count:(i + 1) * count, :] = jnp.where(
            index < ends[0], ref[...].astype(F32), 0.0
        ).astype(BF16)


def masked(pieces, ends):
    rows, width = pieces[0].shape
    return pl.pallas_call(
        masked_body,
        in_specs=[IN_SMEM] + [IN_VMEM] * len(pieces),
        out_specs=IN_VMEM,
        out_shape=jax.ShapeDtypeStruct((rows * len(pieces), width), BF16),
        compiler_params=pltpu.CompilerParams(vmem_limit_bytes=VMEM_LIMIT),
        name="masked",
    )(ends, *pieces)


def on_device(
    enc_tokens,
    src_lengths,
    enc_gain,
    enc_query,
    enc_key,
    enc_value,
    enc_output,
    enc_bias,
    mem_gain,
    dec_tokens,
    tgt_lengths,
    lang_tags,
    lang_table,
    cross_gain,
    cross_query,
    cross_key,
    cross_value,
    cross_output,
    ffn_gain,
    ffn_in,
    ffn_out,
):
    groups = lax.axis_size("dp")
    size = lax.axis_size("tensor")
    per_pair = size // groups
    src_len = enc_tokens.shape[1]
    target_len = dec_tokens.shape[1]

    to_source = []
    for row in range(groups * size):
        j, m = row // size, row % size
        to_source.append((row, (m // per_pair) * size + (m % per_pair) * groups + j))
    to_home = [(b, a) for a, b in to_source]

    *enc_weights, bias = load(
        [enc_query, enc_key, enc_value, enc_output], enc_bias, src_len, src_len
    )
    sent = decoder_rows(dec_tokens[0], lang_table, lang_tags)
    if OPT["home"] != "free":
        sent = after(sent, enc_weights[0])
    arrived = lax.ppermute(sent, ("dp", "tensor"), to_source)
    dec_rows = arrived[:target_len]
    dec_lang = jnp.broadcast_to(arrived[target_len:target_len + 1], dec_rows.shape)
    dec_normed, dec_input = norm_sum([dec_rows, dec_lang], cross_gain, 1, True)
    def enc_run(k, rows):
        return self_attention(src_lengths, 2 * k, rows, enc_weights, bias, enc_gain[None, :])

    dec_slots, done = [], {}
    stacks = [[cross_query, cross_key, cross_value, cross_output]]
    if cross_query.shape != cross_output.shape:
        stacks = [stacks[0][:3], stacks[0][3:]]
    cross_own = [load_stack(weights) for weights in stacks]
    if OPT["ls"] == 0:
        enc_weights[0] = after(enc_weights[0], *cross_own)

    def hook(out):
        rows = after(dec_normed, out) if OPT["dtie"] else dec_normed
        dec_slots.extend(spread(rows))
        wanted = [dec_slots[1], dec_slots[size // 4]]
        before = {2: [dec_normed]} if OPT["norm2"] else {}
        late = []
        before[OPT["ls"]] = before.get(OPT["ls"], []) + cross_own
        if OPT["dec"] == "early":
            before[1] = before.get(1, []) + wanted[:1]
            before[size // 2 - 1] = before.get(size // 2 - 1, []) + wanted[1:]
        elif OPT["dec"] == "last":
            before[size // 2 - 1] = before.get(size // 2 - 1, []) + wanted
        elif OPT["dec"] == "late":
            late = wanted
        return before, late

    enc_terms = exchange("enc", enc_tokens[0], enc_run, True, hook, done)
    memory_out, enc_memory = norm_sum([enc_tokens[0]] + enc_terms, mem_gain, 2, False)

    last_sums = [*done.values(), enc_terms[1]] if OPT["w"] == "all" else [*done.values()]
    if OPT["w"] == "got":
        last_sums.append(enc_terms[2])
    cross_other = [swap(after(stack, *last_sums), 1) for stack in cross_own]

    def cross_run(k, rows):
        return cross_attention(src_lengths, 2 * k, rows, dec_slots[k], cross_own, cross_other)

    cross_terms = exchange("mem", enc_memory, cross_run, False)
    ffn_normed, hidden = norm_sum([dec_input] + cross_terms, ffn_gain, 1, True)

    def ffn_pair(k, blocks):
        return ffn(blocks, ffn_in, ffn_out)

    ffn_terms = exchange("ffn", ffn_normed, ffn_pair, True, straight=OPT["straight"])

    if OPT["straight"]:
        ffn_terms, far_terms = ffn_terms
        pieces = []
        step = target_len // OPT["pieces"]
        for start in range(0, target_len, step):
            rows = slice(start, start + step)
            terms = [term[rows] for term in (hidden, *ffn_terms)]
            terms += [swap(term[rows], 2 * k) for k, term in far_terms.items()]
            pieces.append(lax.ppermute(bf16_sum(*terms), ("dp", "tensor"), to_home))
    else:
        pieces = [lax.ppermute(bf16_sum(hidden, *ffn_terms), ("dp", "tensor"), to_home)]
    dec_out = masked(pieces, tgt_lengths)
    return (memory_out[None], dec_out[None])


def solution(mesh):
    in_specs = (
        P(("dp", "tensor"), None, None),
        P(),
        P(),
        P(None, "tensor"),
        P(None, "tensor"),
        P(None, "tensor"),
        P("tensor", None),
        P("tensor", None),
        P(),
        P(("dp", "tensor"), None, None),
        P(("dp", "tensor")),
        P("dp"),
        P(),
        P(),
        P(None, "tensor"),
        P(None, "tensor"),
        P(None, "tensor"),
        P("tensor", None),
        P(),
        P(None, "tensor"),
        P("tensor", None),
    )
    out_specs = (P(("dp", "tensor"), None, None), P(("dp", "tensor"), None, None))
    return jax.shard_map(
        on_device, mesh=mesh, in_specs=in_specs, out_specs=out_specs, check_vma=False
    )
```
